32 devices in a mesh: groups: 2 (over y), adapter: 8 (over z, x), tensor: 2 (over core).
Axes of the slice: x: 2, y: 2, z: 4, core: 2. Of those that a mesh axis runs over, the one named last changes fastest.
Arguments:
- attended: bfloat16 [128, 8192], P(('groups', 'adapter'), 'tensor'), parts along dimension 0, may hold values from -6 to 6
- adapter_index_rows: int32 [128, 1], P(('groups', 'adapter')), parts along dimension 0, may hold values from 0 to 15; in each aligned block of 64 rows (0 to 63, 64 to 127, ...) at most 8 rows name the same one
- output_weight: bfloat16 [8192, 8192], P('adapter', 'tensor'), may hold values from -0.0625 to 0.0625
- adapter_down_weight: bfloat16 [16, 64, 8192], P('adapter', None, 'tensor'), may hold values from -0.0625 to 0.0625
- adapter_up_weight: bfloat16 [8192, 1024], P('adapter', 'tensor'), may hold values from -0.75 to 0.75
Outputs:
- projected: bfloat16 [128, 8192], P(('groups', 'adapter'), 'tensor'), parts along dimension 0
The draws below stay inside these ranges and needn't reach their ends.
There are 2 independent parts, one for each index of `groups`. The reference program is written for one: setup_inputs(seed, part) draws one part's arguments, and reference() takes and returns one part's arrays. A program takes and returns all parts, laid end to end along the dimension named above; an argument that names none is the same for every part. Nothing has to cross between parts.
Inputs may be any that keep to these rules, and one draw needn't show every extreme that they name: `adapter_index_rows`: no adapter is named by more than 8 rows of one part; one adapter is named by exactly 8; every adapter is named by some row.
All inputs are finite; a program needn't handle non-finite values.
Results may differ from the reference program's by a relative error of at most 0.0047.
Values may be sent and summed in bfloat16 or wider, within the bound.
No kernel may reach another device: no remote copies, remote signals or barrier semaphores. Data moves between devices by JAX's collectives and lax.ppermute only.
A program may use at most 64 MiB of HBM per device.

```python
import math
import jax
import jax.numpy as jnp
import numpy as np
from jax import lax

MODEL_WIDTH = 8192
ADAPTER_RANK = 64
AD_DEV = 2
ADAPTER_TOTAL = 16
ROWS = 64
MOST = 8
N_ADAPTER = 8


def shard_levels(own_key, extent, shards, low, top_value):
    level = 1.0
    for position, parts in shards:
        steps = jax.random.uniform(jax.random.fold_in(jax.random.fold_in(own_key, 6), position), (parts,), jnp.float32, low / len(shards), top_value / len(shards))
        level = level * jnp.repeat(jnp.exp(steps), extent[position] // parts).reshape((-1,) + (1,) * (len(extent) - 1 - position))
    return level


def deal_out(stream_key, own, number, rows, amount, top, reach, skew):
    ranking = jax.random.permutation(stream_key, amount)
    heavy_load, ordinary = load_shares(amount, rows * top, reach, skew, True), load_shares(amount, rows * top, reach, skew, False)
    places = jnp.arange(amount)

    def named(lengths, offset_by):
        used = int((lengths > 0).sum())
        fixed = max(1, used // 4)
        moved = fixed + (places - fixed + offset_by * (used - fixed)) % max(1, amount - fixed)
        return jnp.zeros((amount,), jnp.int32).at[ranking[jnp.where(places < fixed, places, moved)]].set(jnp.asarray(lengths, jnp.int32))

    lengths = jnp.where(number % 4 == 0, named(heavy_load, number // 4), named(ordinary, number - number // 4 - 1))
    mixed = jax.random.permutation(jax.random.fold_in(own, 3), amount)
    source_of, sink = mixed[0:amount // 2 * 2:2], mixed[1:amount // 2 * 2:2]
    slack = jnp.minimum(lengths[source_of] - 1, reach - lengths[sink]) // 2
    slack = jnp.where((source_of == ranking[0]) | (sink == ranking[0]) | (lengths[sink] == 0), 0, jnp.maximum(slack, 0))
    moved = jax.random.randint(jax.random.fold_in(own, 4), (amount // 2,), 0, 1 << 20) % (slack + 1)
    lengths = lengths.at[source_of].add(-moved).at[sink].add(moved)
    members = jnp.searchsorted(jnp.cumsum(lengths), jnp.arange(rows * top), side="right").astype(jnp.int32)
    grid = members.reshape(top, rows).T
    grid = grid[jax.random.permutation(jax.random.fold_in(own, 1), rows)]
    offset_by = jax.random.randint(jax.random.fold_in(own, 2), (rows, 1), 0, top)
    return jnp.take_along_axis(grid, (jnp.arange(top)[None, :] + offset_by) % top, axis=1)


def load_shares(number_of, total, reach, skew, full):
    loads = [(1 << 20) // math.isqrt(grade ** skew) + 1 for grade in range(1, number_of + 1)]
    largest = reach if full else min(reach, max(-(-total // number_of), total * loads[0] // sum(loads)))
    least = 1 if total - largest >= number_of - 1 else 0
    holding, spare = [largest] + [least] * (number_of - 1), total - largest - least * (number_of - 1)
    while spare > 0:
        candidates = [i for i in range(1, number_of) if holding[i] < largest] or [i for i in range(1, number_of) if holding[i] < reach]
        mass, left = sum([loads[i] for i in candidates]), spare
        for i in candidates:
            addition = min(reach - holding[i], max(1, left * loads[i] // mass), spare)
            holding[i] = holding[i] + addition
            spare = spare - addition
    return np.array(holding)


def normal_values(stream_key, extent, spread, reach, pieces=(), held_as=jnp.bfloat16):
    drawn = jax.random.normal(stream_key, extent, jnp.float32) * spread
    if len(pieces) > 0:
        drawn = shard_levels(stream_key, extent, pieces, -0.22, 0.18) * drawn
    return jnp.clip(drawn, min=-reach, max=reach).astype(held_as)


def setup_inputs(seed: int = 0, part: int = 0) -> dict:
    seeds = jax.random.split(jax.random.key(seed), 6)
    part_splits = jax.random.split(jax.random.fold_in(seeds[5], part), 6)
    attended = normal_values(part_splits[0], (ROWS, MODEL_WIDTH), 1.0, 6.0, ((0, 8), (1, 2)))
    adapter_index_rows_keys = jax.random.split(jax.random.fold_in(part_splits[1], 1), ROWS // ROWS)
    adapter_index_rows_turns = jax.random.permutation(jax.random.fold_in(part_splits[1], 3), ROWS // ROWS)
    adapter_index_rows = jax.vmap(lambda own, number: deal_out(jax.random.fold_in(part_splits[1], 2), own, number, ROWS, AD_DEV * N_ADAPTER, 1, MOST, 2))(adapter_index_rows_keys, adapter_index_rows_turns).reshape((ROWS, 1))
    output_weight = normal_values(seeds[2], (MODEL_WIDTH, MODEL_WIDTH), MODEL_WIDTH ** -0.5, 0.0625, ((0, 8), (1, 2)))
    adapter_down_weight = normal_values(seeds[3], (ADAPTER_TOTAL, ADAPTER_RANK, MODEL_WIDTH), MODEL_WIDTH ** -0.5, 0.0625, ((0, 8), (2, 2)))
    adapter_up_weight = normal_values(seeds[4], (MODEL_WIDTH, ADAPTER_TOTAL * ADAPTER_RANK), ADAPTER_RANK ** -0.5, 0.75, ((0, 8), (1, 2)))
    return {"attended": attended, "adapter_index_rows": adapter_index_rows, "output_weight": output_weight, "adapter_down_weight": adapter_down_weight, "adapter_up_weight": adapter_up_weight}


adapter_scale = 2.0


def reference(attended, adapter_index_rows, output_weight, adapter_down_weight, adapter_up_weight):
    base_output = lax.dot_general(attended, output_weight, (((1,), (1,)), ((), ())), preferred_element_type=jnp.float32)
    row_ids = adapter_index_rows[:, 0].astype(jnp.int32)
    batch_rows = row_ids.shape[0]
    block = min(batch_rows, 64)
    input_blocks = attended.reshape(batch_rows // block, block, attended.shape[1])
    index_block_list = row_ids.reshape(batch_rows // block, block)
    up_weight_cube = adapter_up_weight.reshape(adapter_up_weight.shape[0], adapter_up_weight.shape[1] // ADAPTER_RANK, ADAPTER_RANK)

    def single_block(pair):
        rows_x, row_index_list = pair
        down_matrix = adapter_down_weight[row_index_list]
        shrunk = jnp.einsum("brd,bd->br", down_matrix.astype(jnp.float32), rows_x.astype(jnp.float32)).astype(jnp.bfloat16)
        upper = up_weight_cube[:, row_index_list, :]
        return jnp.einsum("dbr,br->bd", upper.astype(jnp.float32), shrunk.astype(jnp.float32))

    adapter_update = lax.map(single_block, (input_blocks, index_block_list)).reshape(batch_rows, adapter_up_weight.shape[0])
    return (base_output + adapter_scale * adapter_update).astype(jnp.bfloat16)
```

```python
import jax
import jax.numpy as jnp
from jax import lax
from jax.sharding import PartitionSpec as P

adapter_scale = 2.0
ID_BASE = 256
ID_LANES = 128


def shards(attended, adapter_index_rows, output_weight, adapter_down_weight, adapter_up_weight):
    per_dev, half_width = attended.shape
    column_width = output_weight.shape[0]
    local_count, rank_width = adapter_down_weight.shape[:2]
    groups_number = adapter_up_weight.shape[1] // rank_width
    me = lax.axis_index("adapter")
    core = lax.axis_index("tensor")
    n = lax.axis_size("adapter")
    cores = lax.axis_size("tensor")
    part = n // cores
    rows = n * per_dev
    f32, bf16 = jnp.float32, jnp.bfloat16

    ids = adapter_index_rows[:, 0]
    digits = jnp.stack([ids // ID_BASE, ids % ID_BASE], axis=1).astype(bf16)
    payload = jnp.concatenate(
        [attended, jnp.pad(digits, ((0, 0), (0, ID_LANES - 2)))], axis=1
    )
    blocks = [payload] + [
        lax.ppermute(payload, "adapter", [(i, (i + d) % n) for i in range(n)]) for d in range(1, n)
    ]
    gathered = jnp.concatenate(blocks, axis=0)
    piece = gathered[:, :half_width]
    all_ids = (
        gathered[:, half_width].astype(jnp.int32) * ID_BASE
        + gathered[:, half_width + 1].astype(jnp.int32)
    )

    shrink = lax.dot_general(
        piece,
        adapter_down_weight.reshape(local_count * rank_width, half_width),
        (((1,), (1,)), ((), ())),
        preferred_element_type=f32,
    ).reshape(rows, local_count, rank_width)
    owned = me * local_count + jnp.arange(local_count, dtype=jnp.int32)
    mine = all_ids[:, None] == owned[None, :]
    shrink = jnp.where(mine[:, :, None], shrink, 0.0).sum(axis=1)

    def pair(i, t):
        return i % n * cores + t

    both = ("adapter", "tensor")
    swap = [(pair(i, t), pair(i, 1 - t)) for i in range(n) for t in range(cores)]
    shrink = (shrink + lax.ppermute(shrink, both, swap)).astype(bf16)
    cube = shrink.reshape(n, per_dev, rank_width)
    shrunk = jnp.zeros((rows, rank_width), bf16)
    for s in range(part):
        sent = jnp.where(core == 0, jnp.roll(cube, s, axis=0), jnp.roll(cube, s + part, axis=0))
        pairs = [
            (pair(i, t), pair(i + s + part * t, i // part)) for i in range(n) for t in range(cores)
        ]
        shrunk = shrunk + lax.ppermute(sent.reshape(rows, rank_width), both, pairs)

    base = lax.dot_general(
        piece, output_weight, (((1,), (1,)), ((), ())), preferred_element_type=f32
    )
    shifted = all_ids - core * groups_number
    hits = (shifted[:, None] == jnp.arange(groups_number, dtype=jnp.int32)[None, :]).astype(bf16)
    expanded = (hits[:, :, None] * shrunk[:, None, :]).reshape(rows, groups_number * rank_width)
    update = lax.dot_general(
        expanded, adapter_up_weight, (((1,), (1,)), ((), ())), preferred_element_type=f32
    )
    partial = (base + adapter_scale * update).reshape(cores, part, per_dev, column_width)
    keep = jnp.where(core == 0, partial[0], partial[1])
    give = jnp.where(core == 0, partial[1], partial[0])
    total = (keep + lax.ppermute(give, both, swap)).astype(bf16)
    pieces = []
    for s in range(part):
        pairs = [
            (pair(i, t), pair(i - s - part * t, i // part)) for i in range(n) for t in range(cores)
        ]
        pieces.append(lax.ppermute(total[s], both, pairs))
    stacked = jnp.concatenate(pieces, axis=1)
    twice = jnp.concatenate([stacked, stacked], axis=1)
    start = (part - me % part) % part * column_width
    return lax.dynamic_slice(twice, (0, start), (per_dev, part * column_width))


def solution(mesh):
    in_specs = (
        P(("groups", "adapter"), "tensor"),
        P(("groups", "adapter"), None),
        P("adapter", "tensor"),
        P("adapter", None, "tensor"),
        P("adapter", "tensor"),
    )
    out_specs = P(("groups", "adapter"), "tensor")
    return jax.shard_map(shards, mesh=mesh, in_specs=in_specs, out_specs=out_specs, check_vma=False)
```

```python
import functools

import jax
import jax.numpy as jnp
from jax import lax
from jax.experimental import pallas as pl
from jax.experimental.pallas import tpu as pltpu
from jax.sharding import PartitionSpec as P

MOST = 8
LANES = 128
ID_BASE = 256

adapter_scale = 2.0

f32, bf16, i32 = jnp.float32, jnp.bfloat16, jnp.int32
NT = (((1,), (1,)), ((), ()))
MIB = 1 << 20


def call(body, outs, args, vmem=4 * MIB, scratch=(), in_vmem=()):
    args = [
        pltpu.with_memory_space_constraint(a, pltpu.VMEM) if i in in_vmem else a
        for i, a in enumerate(args)
    ]
    return pl.pallas_call(
        body,
        out_shape=outs,
        in_specs=[pl.BlockSpec(memory_space=pltpu.VMEM)] * len(args),
        out_specs=jax.tree.map(lambda _: pl.BlockSpec(memory_space=pltpu.VMEM), outs),
        scratch_shapes=list(scratch),
        compiler_params=pltpu.CompilerParams(vmem_limit_bytes=vmem),
    )(*args)


def shape(*dims, dtype=f32):
    return jax.ShapeDtypeStruct(dims, dtype)


def iota(dims, axis):
    return lax.broadcasted_iota(i32, dims, axis)


def pack_kernel(att_ref, ids_ref, out_ref):
    per_dev, width = att_ref.shape
    here = iota((per_dev, per_dev), 0) == iota((per_dev, per_dev), 1)
    ids = jnp.sum(jnp.where(here, ids_ref[...], 0), axis=1, keepdims=True)
    lane = iota((per_dev, LANES), 1)
    digits = jnp.where(lane == 0, ids >> 8, jnp.where(lane == 1, ids & (ID_BASE - 1), 0))
    out_ref[:, :width] = att_ref[...]
    out_ref[:, width:] = digits.astype(f32).astype(bf16)


def shrink_kernel(n, local, *refs):
    blocks, (down_ref, x_ref, meta_ref, slots_ref) = refs[:n], refs[n:]
    per_dev = blocks[0].shape[0]
    width = x_ref.shape[1]
    rows = n * per_dev
    me = lax.axis_index("adapter")
    whole = jnp.concatenate([b[...].astype(f32) for b in blocks], axis=0)
    x_ref[...] = whole[:, :width].astype(bf16)
    product = lax.dot_general(x_ref[...], down_ref[...], NT, preferred_element_type=f32)
    digits = whole[:, width:]
    lane = iota((rows, LANES), 1)
    ids = jnp.sum(
        jnp.where(lane == 0, digits * ID_BASE, jnp.where(lane == 1, digits, 0.0)),
        axis=1,
        keepdims=True,
    ).astype(i32)
    square = (rows, rows)
    diagonal = iota(square, 0) == iota(square, 1)

    def home(which):
        return (me + n - which // per_dev) % n * per_dev + which % per_dev

    ids_across = jnp.sum(jnp.where(diagonal, ids, 0), axis=0, keepdims=True)
    same = ids == ids_across
    down_order, across_order = home(iota(square, 0)), home(iota(square, 1))
    rank = jnp.sum((same & (across_order < down_order)).astype(i32), axis=1, keepdims=True)
    rank_across = jnp.sum((same & (down_order < across_order)).astype(i32), axis=0, keepdims=True)
    meta_ref[...] = jnp.where(lane == 0, ids, rank)
    rank_width = down_ref.shape[0] // local
    slots = jnp.zeros((MOST, local * rank_width), f32)
    slot_lane = iota(slots.shape, 1)
    for k in range(local):
        picks = (rank_across == iota((MOST, rows), 0)) & (ids_across == me * local + k)
        found = jnp.dot(
            picks.astype(f32), product, precision=lax.Precision.HIGHEST, preferred_element_type=f32
        )
        slots = jnp.where(slot_lane // rank_width == k, found, slots)
    for j in range(slots_ref.shape[0]):
        slots_ref[j] = slots


def base_kernel(x_ref, weight_ref, out_ref):
    out_ref[...] = lax.dot_general(x_ref[...], weight_ref[...], NT, preferred_element_type=f32)


def expand_kernel(n, cores, local, rank_width, base_ref, meta_ref, slots_ref, up_ref, out_ref):
    part = n // cores
    rows = base_ref.shape[0]
    per_dev = rows // n
    me, core = lax.axis_index("adapter"), lax.axis_index("tensor")
    first = core * part
    owners = []
    for j in range(part):
        at = (first + j) * cores
        owners.append(sum(slots_ref[at + t] for t in range(1, cores)) + slots_ref[at])
    table = jnp.concatenate(owners, axis=1).astype(bf16)
    ids, rank = meta_ref[:, :1], meta_ref[:, 1:2]
    picks = (rank == iota((rows, MOST), 1)).astype(f32).astype(bf16)
    spread = jnp.dot(picks, table, preferred_element_type=f32)
    wanted = iota(spread.shape, 1) // rank_width + first * local
    spread = jnp.where(ids == wanted, spread, 0.0).astype(bf16)
    update = lax.dot_general(spread, up_ref[...], NT, preferred_element_type=f32)
    total = base_ref[...] + adapter_scale * update
    for d in range(n):
        out_ref[(me + n - d) % n] = total[d * per_dev : (d + 1) * per_dev]


def pair_kernel(mine_ref, other_ref, out_ref):
    out_ref[...] = (mine_ref[...] + other_ref[...]).astype(bf16)


def join_kernel(part, blocks_ref, out_ref):
    first = lax.axis_index("tensor") * part
    width = blocks_ref.shape[2]
    for j in range(part):
        out_ref[:, j * width : (j + 1) * width] = blocks_ref[first + j]


def shards(attended, adapter_index_rows, output_weight, adapter_down_weight, adapter_up_weight):
    per_dev, half_width = attended.shape
    column_width = output_weight.shape[0]
    local, rank_width = adapter_down_weight.shape[:2]
    n = lax.axis_size("adapter")
    cores = lax.axis_size("tensor")
    part = n // cores
    rows = n * per_dev
    both = ("adapter", "tensor")

    payload = call(
        pack_kernel,
        shape(per_dev, half_width + LANES, dtype=bf16),
        [attended, adapter_index_rows.reshape(1, per_dev)],
    )
    blocks = [payload] + [
        lax.ppermute(payload, "adapter", [(i, (i + d) % n) for i in range(n)]) for d in range(1, n)
    ]
    down = adapter_down_weight.reshape(local * rank_width, half_width)
    piece, meta, slots = call(
        functools.partial(shrink_kernel, n, local),
        (
            shape(rows, half_width, dtype=bf16),
            shape(rows, LANES, dtype=i32),
            shape(n * cores, MOST, local * rank_width),
        ),
        blocks + [down],
        vmem=16 * MIB,
    )
    slots = lax.all_to_all(slots, both, split_axis=0, concat_axis=0, tiled=True)
    base = call(
        base_kernel,
        shape(rows, column_width),
        [piece, output_weight],
        vmem=16 * MIB,
        in_vmem=(1,),
    )
    partial = call(
        functools.partial(expand_kernel, n, cores, local, rank_width),
        shape(n, per_dev, column_width),
        [base, meta, slots, adapter_up_weight],
        vmem=16 * MIB,
    )
    swap = [(i * cores + t, i * cores + 1 - t) for i in range(n) for t in range(cores)]
    other = lax.ppermute(partial, both, swap)
    total = call(pair_kernel, shape(n, per_dev, column_width, dtype=bf16), [partial, other])
    received = lax.all_to_all(total, "adapter", split_axis=0, concat_axis=0, tiled=True)
    return call(
        functools.partial(join_kernel, part),
        shape(per_dev, part * column_width, dtype=bf16),
        [received],
    )


def solution(mesh):
    in_specs = (
        P(("groups", "adapter"), "tensor"),
        P(("groups", "adapter"), None),
        P("adapter", "tensor"),
        P("adapter", None, "tensor"),
        P("adapter", "tensor"),
    )
    out_specs = P(("groups", "adapter"), "tensor")
    return jax.shard_map(shards, mesh=mesh, in_specs=in_specs, out_specs=out_specs, check_vma=False)
```

```python
import functools

import jax
import jax.numpy as jnp
from jax import lax
from jax.experimental import pallas as pl
from jax.experimental.pallas import tpu as pltpu
from jax.sharding import PartitionSpec as P

MOST = 8
LANES = 128
ID_BASE = 256
AHEAD = 40_000_000_000

adapter_scale = 2.0

f32, bf16, i32 = jnp.float32, jnp.bfloat16, jnp.int32
NT = (((1,), (1,)), ((), ()))
MIB = 1 << 20


def call(body, outs, args, vmem=4 * MIB, scratch=(), in_vmem=(), in_hbm=(), flops=0):
    args = [
        pltpu.with_memory_space_constraint(
            a, pltpu.VMEM if i in in_vmem else pltpu.HBM if i in in_hbm else pl.ANY
        )
        for i, a in enumerate(args)
    ]
    return pl.pallas_call(
        body,
        out_shape=outs,
        in_specs=[
            pl.BlockSpec(memory_space=pltpu.HBM if i in in_hbm else pltpu.VMEM)
            for i in range(len(args))
        ],
        out_specs=jax.tree.map(lambda _: pl.BlockSpec(memory_space=pltpu.VMEM), outs),
        scratch_shapes=list(scratch),
        compiler_params=pltpu.CompilerParams(vmem_limit_bytes=vmem),
        cost_estimate=pl.CostEstimate(flops=flops, bytes_accessed=flops // 100, transcendentals=0)
        if flops
        else None,
    )(*args)


def shape(*dims, dtype=f32):
    return jax.ShapeDtypeStruct(dims, dtype)


def iota(dims, axis):
    return lax.broadcasted_iota(i32, dims, axis)


def pack_kernel(att_hbm, ids_hbm, out_ref, att_ref, ids_ref, sems):
    copies = [
        pltpu.make_async_copy(att_hbm, att_ref, sems.at[0]),
        pltpu.make_async_copy(ids_hbm, ids_ref, sems.at[1]),
    ]
    for c in copies:
        c.start()
    for c in copies:
        c.wait()
    per_dev, width = att_ref.shape
    here = iota((per_dev, per_dev), 0) == iota((per_dev, per_dev), 1)
    ids = jnp.sum(jnp.where(here, ids_ref[...], 0), axis=1, keepdims=True)
    lane = iota((per_dev, LANES), 1)
    digits = jnp.where(lane == 0, ids >> 8, jnp.where(lane == 1, ids & (ID_BASE - 1), 0))
    out_ref[:, :width] = att_ref[...]
    out_ref[:, width:] = digits.astype(f32).astype(bf16)


def shrink_kernel(n, local, *refs):
    blocks, (down_ref, x_ref, meta_ref, slots_ref) = refs[:n], refs[n:]
    per_dev = blocks[0].shape[0]
    width = x_ref.shape[1]
    rows = n * per_dev
    me = lax.axis_index("adapter")
    whole = jnp.concatenate([b[...].astype(f32) for b in blocks], axis=0)
    x_ref[...] = whole[:, :width].astype(bf16)
    product = lax.dot_general(x_ref[...], down_ref[...], NT, preferred_element_type=f32)
    digits = whole[:, width:]
    lane = iota((rows, LANES), 1)
    ids = jnp.sum(
        jnp.where(lane == 0, digits * ID_BASE, jnp.where(lane == 1, digits, 0.0)),
        axis=1,
        keepdims=True,
    ).astype(i32)
    square = (rows, rows)
    diagonal = iota(square, 0) == iota(square, 1)

    def home(which):
        return ((which // per_dev) ^ me) * per_dev + which % per_dev

    ids_across = jnp.sum(jnp.where(diagonal, ids, 0), axis=0, keepdims=True)
    same = ids == ids_across
    down_order, across_order = home(iota(square, 0)), home(iota(square, 1))
    rank = jnp.sum((same & (across_order < down_order)).astype(i32), axis=1, keepdims=True)
    rank_across = jnp.sum((same & (down_order < across_order)).astype(i32), axis=0, keepdims=True)
    meta_ref[...] = jnp.where(lane == 0, ids, rank)
    rank_width = down_ref.shape[0] // local
    slots = jnp.zeros((MOST, local * rank_width), f32)
    slot_lane = iota(slots.shape, 1)
    for k in range(local):
        picks = (rank_across == iota((MOST, rows), 0)) & (ids_across == me * local + k)
        found = jnp.dot(
            picks.astype(f32), product, precision=lax.Precision.HIGHEST, preferred_element_type=f32
        )
        slots = jnp.where(slot_lane // rank_width == k, found, slots)
    slots_ref[...] = slots


def base_kernel(place, x_ref, weight_ref, out_ref):
    width = out_ref.shape[1]
    out_ref[...] = lax.dot_general(
        x_ref[...],
        weight_ref[place * width : (place + 1) * width, :],
        NT,
        preferred_element_type=f32,
    )


def slots_kernel(mine_ref, other_ref, out_ref):
    out_ref[...] = (mine_ref[...] + other_ref[...]).astype(bf16).astype(f32)


def expand_kernel(n, cores, local, rank_width, *refs):
    part = n // cores
    owners, (base_a, base_b, meta_ref, up_ref, keep_ref, give_ref, spread_ref) = (
        refs[:part],
        refs[part:],
    )
    rows = base_a.shape[0]
    me, core = lax.axis_index("adapter"), lax.axis_index("tensor")
    ids, rank = meta_ref[:, :1], meta_ref[:, 1:2]
    picks = (rank == iota((rows, MOST), 1)).astype(f32).astype(bf16)
    wide = local * rank_width
    for m in range(part):
        low = (me ^ m) % part
        spread = jnp.dot(picks, owners[m][...].astype(bf16), preferred_element_type=f32)
        wanted = iota(spread.shape, 1) // rank_width + (core * part + low) * local
        at = pl.ds(pl.multiple_of(low * wide, wide), wide)
        spread_ref[:, at] = jnp.where(ids == wanted, spread, 0.0).astype(bf16)
    update = adapter_scale * lax.dot_general(
        spread_ref[...], up_ref[...], NT, preferred_element_type=f32
    )
    half = base_a.shape[1]
    near = core == me // part

    def put(keep, give):
        for e, out_ref in ((keep, keep_ref), (give, give_ref)):
            at = slice(e * rows // cores, (e + 1) * rows // cores)
            lead = out_ref.shape[:2]
            out_ref[:, :, :half] = (base_a[at] + update[at, :half]).reshape(*lead, half)
            out_ref[:, :, half:] = (base_b[at] + update[at, half:]).reshape(*lead, half)

    @pl.when(near)
    def _():
        put(0, 1)

    @pl.when(jnp.logical_not(near))
    def _():
        put(1, 0)


def pair_kernel(mine_ref, other_ref, *out_refs):
    for m, out_ref in enumerate(out_refs):
        out_ref[...] = (mine_ref[m] + other_ref[m]).astype(bf16)


def join_kernel(part, *refs):
    pieces, out_ref = refs[:part], refs[part]
    low = lax.axis_index("adapter") % part
    width = pieces[0].shape[1]
    for m in range(part):
        out_ref[:, pl.ds(pl.multiple_of((low ^ m) * width, width), width)] = pieces[m][...]


def shards(attended, adapter_index_rows, output_weight, adapter_down_weight, adapter_up_weight):
    per_dev, half_width = attended.shape
    column_width = output_weight.shape[0]
    local, rank_width = adapter_down_weight.shape[:2]
    n = lax.axis_size("adapter")
    cores = lax.axis_size("tensor")
    part = n // cores
    rows = n * per_dev
    both = ("adapter", "tensor")

    payload = call(
        pack_kernel,
        shape(per_dev, half_width + LANES, dtype=bf16),
        [attended, adapter_index_rows.reshape(1, per_dev)],
        in_hbm=(0, 1),
        flops=AHEAD,
        scratch=[
            pltpu.VMEM((per_dev, half_width), bf16),
            pltpu.VMEM((1, per_dev), i32),
            pltpu.SemaphoreType.DMA((2,)),
        ],
    )
    blocks = [payload] * n
    for e in [*range(2, n, 2), *range(1, n, 2)]:
        if e % 2 == 0:
            blocks[e] = lax.ppermute(payload, "adapter", [(i, i ^ e) for i in range(n)])
        else:
            blocks[e] = lax.ppermute(blocks[e - 1], "adapter", [(i, i ^ 1) for i in range(n)])
    down = adapter_down_weight.reshape(local * rank_width, half_width)
    piece, meta, slots = call(
        functools.partial(shrink_kernel, n, local),
        (
            shape(rows, half_width, dtype=bf16),
            shape(rows, LANES, dtype=i32),
            shape(MOST, local * rank_width),
        ),
        blocks + [down],
        vmem=16 * MIB,
    )
    swap = [(i * cores + t, i * cores + 1 - t) for i in range(n) for t in range(cores)]
    hops = []
    for m in range(part):
        pairs = []
        for i in range(n):
            half = i // part
            pairs.append((i * cores + half, (i ^ m) * cores + half))
            pairs.append((i * cores + 1 - half, (i ^ part ^ m) * cores + half))
        hops.append(pairs)
    base = [
        call(
            functools.partial(base_kernel, place),
            shape(rows, column_width // 2),
            [piece, output_weight],
            vmem=16 * MIB,
            in_vmem=(1,),
            flops=rows * column_width * half_width,
        )
        for place in range(2)
    ]
    other_slots = lax.ppermute(slots, both, swap)
    slots = call(slots_kernel, shape(MOST, local * rank_width), [slots, other_slots])
    owners = [lax.ppermute(slots, both, pairs) for pairs in hops]
    kept = shape(part, per_dev, column_width)
    keep, give = call(
        functools.partial(expand_kernel, n, cores, local, rank_width),
        (kept, kept),
        [*owners, *base, meta, adapter_up_weight],
        vmem=16 * MIB,
        scratch=[pltpu.VMEM((rows, part * local * rank_width), bf16)],
    )
    other = lax.ppermute(give, both, swap)
    sums = call(
        pair_kernel,
        (shape(per_dev, column_width, dtype=bf16),) * part,
        [keep, other],
    )
    pieces = [lax.ppermute(v, both, pairs) for v, pairs in zip(sums, hops)]
    return call(
        functools.partial(join_kernel, part),
        shape(per_dev, part * column_width, dtype=bf16),
        pieces,
    )


def wide_shards(attended, adapter_index_rows, output_weight, adapter_down_weight, adapter_up_weight):
    per_dev = attended.shape[0]
    column_width = output_weight.shape[0]
    local_count = adapter_down_weight.shape[0]
    rank_width = adapter_down_weight.shape[1]
    owner = lax.axis_index("adapter")
    width_all = lax.axis_size("adapter")
    batch_rows = per_dev * width_all
    all_ids = lax.all_gather(adapter_index_rows, "adapter", axis=0, tiled=True)[:, 0]
    owned = owner * local_count + jnp.arange(local_count, dtype=jnp.int32)
    mine = (all_ids[None, :] == owned[:, None]).astype(jnp.int32)
    order_rank = jnp.cumsum(mine, axis=1) - 1
    slot_numbers = jnp.arange(MOST, dtype=jnp.int32)
    chosen = (mine[:, None, :] == 1) & (order_rank[:, None, :] == slot_numbers[None, :, None])
    chosen_half = chosen.astype(jnp.bfloat16)
    piece = lax.all_gather(attended, "adapter", axis=0, tiled=True)
    product = lax.dot_general(
        piece, output_weight, (((1,), (1,)), ((), ())), preferred_element_type=jnp.float32
    )
    base_portion = product
    selected_rows = jnp.einsum(
        "ksn,nd->ksd", chosen_half, piece, preferred_element_type=jnp.float32
    ).astype(jnp.bfloat16)
    shrink_portion = jnp.einsum(
        "oij,omj->oim", selected_rows, adapter_down_weight, preferred_element_type=jnp.float32
    )
    base_portion, shrink_portion = (base_portion, shrink_portion)
    spread_rows = jnp.einsum(
        "ksn,ksr->nr", chosen.astype(jnp.float32), shrink_portion, precision=lax.Precision.HIGHEST
    )
    shrunk = lax.psum(spread_rows, ("adapter", "tensor")).astype(jnp.bfloat16)
    tensor_place = lax.axis_index("tensor")
    groups_number = adapter_up_weight.shape[1] // rank_width
    shifted = all_ids - tensor_place * groups_number
    block = min(batch_rows, 256)

    def expand(pair):
        ids_block, shrunk_block = pair
        hits = (ids_block[:, None] == jnp.arange(groups_number, dtype=jnp.int32)[None, :]).astype(
            jnp.bfloat16
        )
        expanded_update = (hits[:, :, None] * shrunk_block[:, None, :]).reshape(
            block, groups_number * rank_width
        )
        return lax.dot_general(
            expanded_update,
            adapter_up_weight,
            (((1,), (1,)), ((), ())),
            preferred_element_type=jnp.float32,
        )

    adapter_update = lax.map(
        expand,
        (
            shifted.reshape(batch_rows // block, block),
            shrunk.reshape(batch_rows // block, block, rank_width),
        ),
    )
    running_partial = base_portion + adapter_scale * adapter_update.reshape(
        batch_rows, column_width
    )
    blocks = lax.all_to_all(running_partial, "adapter", split_axis=0, concat_axis=1, tiled=True)
    total = lax.psum_scatter(blocks, "tensor", scatter_dimension=1, tiled=True)
    return total.astype(jnp.bfloat16)


def solution(mesh):
    sizes = mesh.shape
    direct = sizes["adapter"] <= 16 and sizes["tensor"] == 2
    in_specs = (
        P(("groups", "adapter"), "tensor"),
        P(("groups", "adapter"), None),
        P("adapter", "tensor"),
        P("adapter", None, "tensor"),
        P("adapter", "tensor"),
    )
    out_specs = P(("groups", "adapter"), "tensor")
    body = shards if direct else wide_shards
    return jax.shard_map(body, mesh=mesh, in_specs=in_specs, out_specs=out_specs, check_vma=False)
```

```python
import functools

import jax
import jax.numpy as jnp
from jax import lax
from jax.experimental import pallas as pl
from jax.experimental.pallas import tpu as pltpu
from jax.sharding import PartitionSpec as P

MOST = 8
LANES = 128
ID_BASE = 256
AHEAD = 40_000_000_000

adapter_scale = 2.0

f32, bf16, i32 = jnp.float32, jnp.bfloat16, jnp.int32
NT = (((1,), (1,)), ((), ()))
MIB = 1 << 20


def call(body, outs, args, vmem=4 * MIB, scratch=(), in_vmem=(), in_hbm=(), flops=0):
    args = [
        pltpu.with_memory_space_constraint(
            a, pltpu.VMEM if i in in_vmem else pltpu.HBM if i in in_hbm else pl.ANY
        )
        for i, a in enumerate(args)
    ]
    return pl.pallas_call(
        body,
        out_shape=outs,
        in_specs=[
            pl.BlockSpec(memory_space=pltpu.HBM if i in in_hbm else pltpu.VMEM)
            for i in range(len(args))
        ],
        out_specs=jax.tree.map(lambda _: pl.BlockSpec(memory_space=pltpu.VMEM), outs),
        scratch_shapes=list(scratch),
        compiler_params=pltpu.CompilerParams(vmem_limit_bytes=vmem),
        cost_estimate=pl.CostEstimate(flops=flops, bytes_accessed=flops // 100, transcendentals=0)
        if flops
        else None,
    )(*args)


def shape(*dims, dtype=f32):
    return jax.ShapeDtypeStruct(dims, dtype)


def iota(dims, axis):
    return lax.broadcasted_iota(i32, dims, axis)


def pack_kernel(att_hbm, ids_hbm, out_ref, att_ref, ids_ref, sems):
    copies = [
        pltpu.make_async_copy(att_hbm, att_ref, sems.at[0]),
        pltpu.make_async_copy(ids_hbm, ids_ref, sems.at[1]),
    ]
    for c in copies:
        c.start()
    for c in copies:
        c.wait()
    per_dev, width = att_ref.shape
    here = iota((per_dev, per_dev), 0) == iota((per_dev, per_dev), 1)
    ids = jnp.sum(jnp.where(here, ids_ref[...], 0), axis=1, keepdims=True)
    lane = iota((per_dev, LANES), 1)
    digits = jnp.where(lane == 0, ids >> 8, jnp.where(lane == 1, ids & (ID_BASE - 1), 0))
    out_ref[:, :width] = att_ref[...]
    out_ref[:, width:] = digits.astype(f32).astype(bf16)


def shrink_kernel(n, local, *refs):
    blocks, (down_ref, x_ref, meta_ref, slots_ref) = refs[:n], refs[n:]
    per_dev = blocks[0].shape[0]
    width = x_ref.shape[1]
    rows = n * per_dev
    me = lax.axis_index("adapter")
    whole = jnp.concatenate([b[...].astype(f32) for b in blocks], axis=0)
    x_ref[...] = whole[:, :width].astype(bf16)
    product = lax.dot_general(x_ref[...], down_ref[...], NT, preferred_element_type=f32)
    digits = whole[:, width:]
    lane = iota((rows, LANES), 1)
    ids = jnp.sum(
        jnp.where(lane == 0, digits * ID_BASE, jnp.where(lane == 1, digits, 0.0)),
        axis=1,
        keepdims=True,
    ).astype(i32)
    square = (rows, rows)
    diagonal = iota(square, 0) == iota(square, 1)

    def home(which):
        return ((which // per_dev) ^ me) * per_dev + which % per_dev

    ids_across = jnp.sum(jnp.where(diagonal, ids, 0), axis=0, keepdims=True)
    same = ids == ids_across
    down_order, across_order = home(iota(square, 0)), home(iota(square, 1))
    rank = jnp.sum((same & (across_order < down_order)).astype(i32), axis=1, keepdims=True)
    rank_across = jnp.sum((same & (down_order < across_order)).astype(i32), axis=0, keepdims=True)
    meta_ref[...] = jnp.where(lane == 0, ids, rank)
    rank_width = down_ref.shape[0] // local
    slots = jnp.zeros((MOST, local * rank_width), f32)
    slot_lane = iota(slots.shape, 1)
    for k in range(local):
        picks = (rank_across == iota((MOST, rows), 0)) & (ids_across == me * local + k)
        found = jnp.dot(
            picks.astype(f32), product, precision=lax.Precision.HIGHEST, preferred_element_type=f32
        )
        slots = jnp.where(slot_lane // rank_width == k, found, slots)
    slots_ref[...] = slots


def base_kernel(place, x_ref, weight_ref, *refs):
    out_ref = refs[-1]
    width = out_ref.shape[1]
    out_ref[...] = lax.dot_general(
        x_ref[...],
        weight_ref[place * width : (place + 1) * width, :],
        NT,
        preferred_element_type=f32,
    )


def round_kernel(mine_ref, other_ref, out_ref):
    out_ref[0] = (mine_ref[...] + other_ref[...]).astype(bf16).astype(f32)


def stack_kernel(*refs):
    out_ref = refs[-1]
    at = 0
    for ref in refs[:-1]:
        out_ref[at : at + ref.shape[0]] = ref[...]
        at += ref.shape[0]


def near_place():
    part = lax.axis_size("adapter") // lax.axis_size("tensor")
    return lax.axis_index("tensor") == lax.axis_index("adapter") // part


def kept_rows(count, near):
    keep = jnp.where(near, 0, count)
    return pl.ds(pl.multiple_of(keep, count), count), pl.ds(
        pl.multiple_of(count - keep, count), count
    )


def split_kernel(*refs):
    parts, (keep_ref, give_ref) = refs[:-2], refs[-2:]
    keep, give = kept_rows(keep_ref.shape[0], near_place())
    at = 0
    for part in parts:
        columns = slice(at, at + part.shape[1])
        keep_ref[:, columns] = part[keep, :]
        give_ref[:, columns] = part[give, :]
        at += part.shape[1]


def update_kernel(n, cores, local, rank_width, *refs):
    low_ref, high_ref, meta_ref, up_ref, other_up_ref, out_ref, spread_ref = refs
    part = n // cores
    rows = out_ref.shape[0]
    me = lax.axis_index("adapter")
    near = near_place()
    keep, _ = kept_rows(rows, near)
    meta = meta_ref[keep, :]
    ids, rank = meta[:, :1], meta[:, 1:2]
    picks = (rank == iota((rows, MOST), 1)).astype(f32).astype(bf16)
    wide = local * rank_width
    for e in range(n):
        half, low = e // part, e % part
        table = (low_ref if half == 0 else high_ref)[low].astype(bf16)
        spread = jnp.dot(picks, table, preferred_element_type=f32)
        wanted = iota(spread.shape, 1) // rank_width + (me ^ e) * local
        place = jnp.where(near, half, 1 - half)
        at = pl.ds(pl.multiple_of((me ^ e) % part * wide, wide), wide)
        spread_ref[place, :, at] = jnp.where(ids == wanted, spread, 0.0).astype(bf16)
    update = lax.dot_general(spread_ref[0], up_ref[...], NT, preferred_element_type=f32)
    update += lax.dot_general(spread_ref[1], other_up_ref[...], NT, preferred_element_type=f32)
    out_ref[...] = adapter_scale * update


def total_kernel(keep_ref, other_ref, update_ref, out_ref):
    per_dev = out_ref.shape[1]
    for e in range(out_ref.shape[0]):
        at = slice(e * per_dev, (e + 1) * per_dev)
        out_ref[e] = (keep_ref[at] + other_ref[at] + update_ref[at]).astype(bf16)


def pick_kernel(places, *refs):
    for i, (which, at) in enumerate(places):
        refs[-1][i] = refs[which][at]


def join_kernel(places, *refs):
    out_ref = refs[-1]
    part = len(places)
    low = lax.axis_index("adapter") % part
    width = refs[0].shape[2]
    for m, (which, at) in enumerate(places):
        columns = pl.ds(pl.multiple_of((low ^ m) * width, width), width)
        out_ref[:, columns] = refs[which][at]


def shards(attended, adapter_index_rows, output_weight, adapter_down_weight, adapter_up_weight):
    per_dev, half_width = attended.shape
    column_width = output_weight.shape[0]
    local, rank_width = adapter_down_weight.shape[:2]
    n = lax.axis_size("adapter")
    cores = lax.axis_size("tensor")
    part = n // cores
    rows = n * per_dev
    both = ("adapter", "tensor")

    payload = call(
        pack_kernel,
        shape(per_dev, half_width + LANES, dtype=bf16),
        [attended, adapter_index_rows.reshape(1, per_dev)],
        in_hbm=(0, 1),
        flops=AHEAD,
        scratch=[
            pltpu.VMEM((per_dev, half_width), bf16),
            pltpu.VMEM((1, per_dev), i32),
            pltpu.SemaphoreType.DMA((2,)),
        ],
    )
    blocks = [payload] * n
    for e in [*range(2, n, 2), *range(1, n, 2)]:
        if e % 2 == 0:
            blocks[e] = lax.ppermute(payload, "adapter", [(i, i ^ e) for i in range(n)])
        else:
            blocks[e] = lax.ppermute(blocks[e - 1], "adapter", [(i, i ^ 1) for i in range(n)])
    down = adapter_down_weight.reshape(local * rank_width, half_width)
    piece, meta, slots = call(
        functools.partial(shrink_kernel, n, local),
        (
            shape(rows, half_width, dtype=bf16),
            shape(rows, LANES, dtype=i32),
            shape(MOST, local * rank_width),
        ),
        blocks + [down],
        vmem=16 * MIB,
    )
    swap = [(i * cores + t, i * cores + 1 - t) for i in range(n) for t in range(cores)]
    other_up = lax.ppermute(adapter_up_weight, both, swap)

    quarters = 4

    def base_part(place, after=()):
        return call(
            functools.partial(base_kernel, place),
            shape(rows, column_width // quarters),
            [piece, output_weight, *after],
            vmem=8 * MIB,
            in_vmem=(1,),
            flops=rows * column_width * half_width,
        )

    wide = local * rank_width
    other_slots = lax.ppermute(slots, both, swap)
    base = [base_part(0)]
    held = call(round_kernel, shape(1, MOST, wide), [slots, other_slots])
    step = 1
    while step < n:
        got = lax.ppermute(held, "adapter", [(i, i ^ step) for i in range(n)])
        if len(base) < quarters:
            base.append(base_part(len(base), [held]))
        if step == part:
            break
        held = call(stack_kernel, shape(2 * step, MOST, wide), [held, got])
        step *= 2

    while len(base) < quarters:
        base.append(base_part(len(base), [held]))
    kept = shape(rows // cores, column_width)
    keep, give = call(split_kernel, (kept, kept), base)
    other = lax.ppermute(give, both, swap)
    update = call(
        functools.partial(update_kernel, n, cores, local, rank_width),
        kept,
        [held, got, meta, adapter_up_weight, other_up],
        vmem=8 * MIB,
        in_vmem=(3, 4),
        scratch=[pltpu.VMEM((cores, rows // cores, part * wide), bf16)],
    )
    total = call(
        total_kernel, shape(part, per_dev, column_width, dtype=bf16), [keep, other, update]
    )
    pairs = []
    for i in range(n):
        half = i // part
        pairs.append((i * cores + half, i * cores + half))
        pairs.append((i * cores + 1 - half, (i ^ part) * cores + half))
    total = lax.ppermute(total, both, pairs)
    arrays, where = [total], {(e, 0): (0, e) for e in range(part)}
    step = 1
    while step < part:
        sent = [k for k in where if k[0] & step]
        picked = call(
            functools.partial(pick_kernel, [where[k] for k in sent]),
            shape(len(sent), per_dev, column_width, dtype=bf16),
            arrays,
        )
        arrays.append(lax.ppermute(picked, "adapter", [(i, i ^ step) for i in range(n)]))
        for i, (e, block) in enumerate(sent):
            del where[(e, block)]
            where[(e ^ step, block ^ step)] = (len(arrays) - 1, i)
        step *= 2
    return call(
        functools.partial(join_kernel, [where[(0, m)] for m in range(part)]),
        shape(per_dev, part * column_width, dtype=bf16),
        arrays,
    )


def wide_shards(attended, adapter_index_rows, output_weight, adapter_down_weight, adapter_up_weight):
    per_dev = attended.shape[0]
    column_width = output_weight.shape[0]
    local_count = adapter_down_weight.shape[0]
    rank_width = adapter_down_weight.shape[1]
    owner = lax.axis_index("adapter")
    width_all = lax.axis_size("adapter")
    batch_rows = per_dev * width_all
    all_ids = lax.all_gather(adapter_index_rows, "adapter", axis=0, tiled=True)[:, 0]
    owned = owner * local_count + jnp.arange(local_count, dtype=jnp.int32)
    mine = (all_ids[None, :] == owned[:, None]).astype(jnp.int32)
    order_rank = jnp.cumsum(mine, axis=1) - 1
    slot_numbers = jnp.arange(MOST, dtype=jnp.int32)
    chosen = (mine[:, None, :] == 1) & (order_rank[:, None, :] == slot_numbers[None, :, None])
    chosen_half = chosen.astype(jnp.bfloat16)
    piece = lax.all_gather(attended, "adapter", axis=0, tiled=True)
    product = lax.dot_general(
        piece, output_weight, (((1,), (1,)), ((), ())), preferred_element_type=jnp.float32
    )
    base_portion = product
    selected_rows = jnp.einsum(
        "ksn,nd->ksd", chosen_half, piece, preferred_element_type=jnp.float32
    ).astype(jnp.bfloat16)
    shrink_portion = jnp.einsum(
        "oij,omj->oim", selected_rows, adapter_down_weight, preferred_element_type=jnp.float32
    )
    base_portion, shrink_portion = (base_portion, shrink_portion)
    spread_rows = jnp.einsum(
        "ksn,ksr->nr", chosen.astype(jnp.float32), shrink_portion, precision=lax.Precision.HIGHEST
    )
    shrunk = lax.psum(spread_rows, ("adapter", "tensor")).astype(jnp.bfloat16)
    tensor_place = lax.axis_index("tensor")
    groups_number = adapter_up_weight.shape[1] // rank_width
    shifted = all_ids - tensor_place * groups_number
    block = min(batch_rows, 256)

    def expand(pair):
        ids_block, shrunk_block = pair
        hits = (ids_block[:, None] == jnp.arange(groups_number, dtype=jnp.int32)[None, :]).astype(
            jnp.bfloat16
        )
        expanded_update = (hits[:, :, None] * shrunk_block[:, None, :]).reshape(
            block, groups_number * rank_width
        )
        return lax.dot_general(
            expanded_update,
            adapter_up_weight,
            (((1,), (1,)), ((), ())),
            preferred_element_type=jnp.float32,
        )

    adapter_update = lax.map(
        expand,
        (
            shifted.reshape(batch_rows // block, block),
            shrunk.reshape(batch_rows // block, block, rank_width),
        ),
    )
    running_partial = base_portion + adapter_scale * adapter_update.reshape(
        batch_rows, column_width
    )
    blocks = lax.all_to_all(running_partial, "adapter", split_axis=0, concat_axis=1, tiled=True)
    total = lax.psum_scatter(blocks, "tensor", scatter_dimension=1, tiled=True)
    return total.astype(jnp.bfloat16)


def solution(mesh):
    sizes = mesh.shape
    direct = sizes["adapter"] <= 16 and sizes["tensor"] == 2
    in_specs = (
        P(("groups", "adapter"), "tensor"),
        P(("groups", "adapter"), None),
        P("adapter", "tensor"),
        P("adapter", None, "tensor"),
        P("adapter", "tensor"),
    )
    out_specs = P(("groups", "adapter"), "tensor")
    body = shards if direct else wide_shards
    return jax.shard_map(body, mesh=mesh, in_specs=in_specs, out_specs=out_specs, check_vma=False)
```

```python
import functools

import jax
import jax.numpy as jnp
from jax import lax
from jax.experimental import pallas as pl
from jax.experimental.pallas import tpu as pltpu
from jax.sharding import PartitionSpec as P

MOST = 8
LANES = 128
ID_BASE = 256
AHEAD = 40_000_000_000

adapter_scale = 2.0

f32, bf16, i32 = jnp.float32, jnp.bfloat16, jnp.int32
NT = (((1,), (1,)), ((), ()))
MIB = 1 << 20


def call(body, outs, args, vmem=4 * MIB, scratch=(), in_vmem=(), in_hbm=(), flops=0):
    args = [
        pltpu.with_memory_space_constraint(
            a, pltpu.VMEM if i in in_vmem else pltpu.HBM if i in in_hbm else pl.ANY
        )
        for i, a in enumerate(args)
    ]
    return pl.pallas_call(
        body,
        out_shape=outs,
        in_specs=[
            pl.BlockSpec(memory_space=pltpu.HBM if i in in_hbm else pltpu.VMEM)
            for i in range(len(args))
        ],
        out_specs=jax.tree.map(lambda _: pl.BlockSpec(memory_space=pltpu.VMEM), outs),
        scratch_shapes=list(scratch),
        compiler_params=pltpu.CompilerParams(vmem_limit_bytes=vmem),
        cost_estimate=pl.CostEstimate(flops=flops, bytes_accessed=flops // 100, transcendentals=0)
        if flops
        else None,
    )(*args)


def shape(*dims, dtype=f32):
    return jax.ShapeDtypeStruct(dims, dtype)


def iota(dims, axis):
    return lax.broadcasted_iota(i32, dims, axis)


def pack_kernel(att_hbm, ids_hbm, out_ref, att_ref, ids_ref, sems):
    copies = [
        pltpu.make_async_copy(att_hbm, att_ref, sems.at[0]),
        pltpu.make_async_copy(ids_hbm, ids_ref, sems.at[1]),
    ]
    for c in copies:
        c.start()
    for c in copies:
        c.wait()
    per_dev, width = att_ref.shape
    here = iota((per_dev, per_dev), 0) == iota((per_dev, per_dev), 1)
    ids = jnp.sum(jnp.where(here, ids_ref[...], 0), axis=1, keepdims=True)
    lane = iota((per_dev, LANES), 1)
    digits = jnp.where(lane == 0, ids >> 8, jnp.where(lane == 1, ids & (ID_BASE - 1), 0))
    out_ref[:, :width] = att_ref[...]
    out_ref[:, width:] = digits.astype(f32).astype(bf16)


def shrink_kernel(n, local, *refs):
    blocks, (down_ref, x_ref, meta_ref, slots_ref) = refs[:n], refs[n + 1 :]
    per_dev = blocks[0].shape[0]
    width = x_ref.shape[1]
    rows = n * per_dev
    me = lax.axis_index("adapter")
    whole = jnp.concatenate([b[...].astype(f32) for b in blocks], axis=0)
    x_ref[...] = whole[:, :width].astype(bf16)
    product = lax.dot_general(x_ref[...], down_ref[...], NT, preferred_element_type=f32)
    digits = whole[:, width:]
    lane = iota((rows, LANES), 1)
    ids = jnp.sum(
        jnp.where(lane == 0, digits * ID_BASE, jnp.where(lane == 1, digits, 0.0)),
        axis=1,
        keepdims=True,
    ).astype(i32)
    square = (rows, rows)
    diagonal = iota(square, 0) == iota(square, 1)

    def home(which):
        return ((which // per_dev) ^ me) * per_dev + which % per_dev

    ids_across = jnp.sum(jnp.where(diagonal, ids, 0), axis=0, keepdims=True)
    same = ids == ids_across
    down_order, across_order = home(iota(square, 0)), home(iota(square, 1))
    rank = jnp.sum((same & (across_order < down_order)).astype(i32), axis=1, keepdims=True)
    rank_across = jnp.sum((same & (down_order < across_order)).astype(i32), axis=0, keepdims=True)
    meta_ref[...] = jnp.where(lane == 0, ids, rank)
    rank_width = down_ref.shape[0] // local
    slots = jnp.zeros((MOST, local * rank_width), f32)
    slot_lane = iota(slots.shape, 1)
    for k in range(local):
        picks = (rank_across == iota((MOST, rows), 0)) & (ids_across == me * local + k)
        found = jnp.dot(
            picks.astype(f32), product, precision=lax.Precision.HIGHEST, preferred_element_type=f32
        )
        slots = jnp.where(slot_lane // rank_width == k, found, slots)
    slots_ref[...] = slots


def base_kernel(place, x_ref, weight_ref, *refs):
    out_ref = refs[-1]
    width = out_ref.shape[1]
    out_ref[...] = lax.dot_general(
        x_ref[...],
        weight_ref[place * width : (place + 1) * width, :],
        NT,
        preferred_element_type=f32,
    )


def round_kernel(mine_ref, other_ref, far_ref, far_other_ref, out_ref):
    out_ref[0] = (mine_ref[...] + other_ref[...]).astype(bf16).astype(f32)
    out_ref[1] = (far_ref[...] + far_other_ref[...]).astype(bf16).astype(f32)


def is_main():
    part = lax.axis_size("adapter") // lax.axis_size("tensor")
    return lax.axis_index("tensor") != lax.axis_index("adapter") // part


def update_kernel(part, local, rank_width, *refs):
    owners = refs[:part]
    meta_ref, up_ref, other_up_ref, out_ref, spread_ref = refs[part:]
    rows = out_ref.shape[0]
    me, core = lax.axis_index("adapter"), lax.axis_index("tensor")
    wide = local * rank_width

    @pl.when(is_main())
    def _():
        ids, rank = meta_ref[:, :1], meta_ref[:, 1:2]
        picks = (rank == iota((rows, MOST), 1)).astype(f32).astype(bf16)
        for e, slots_ref in enumerate(owners):
            for far in range(slots_ref.shape[0]):
                owner = me ^ (e + far * part)
                spread = jnp.dot(picks, slots_ref[far].astype(bf16), preferred_element_type=f32)
                wanted = iota(spread.shape, 1) // rank_width + owner * local
                at = pl.ds(pl.multiple_of(owner % part * wide, wide), wide)
                spread = jnp.where(ids == wanted, spread, 0.0).astype(bf16)
                spread_ref[owner // part, :, at] = spread
        update = lax.dot_general(spread_ref[core], up_ref[...], NT, preferred_element_type=f32)
        update += lax.dot_general(
            spread_ref[1 - core], other_up_ref[...], NT, preferred_element_type=f32
        )
        out_ref[...] = adapter_scale * update


def total_kernel(count, *refs):
    mine, others, (update_ref, far_ref, *near_refs) = (
        refs[:count],
        refs[count : 2 * count],
        refs[2 * count :],
    )
    part, per_dev, _ = far_ref.shape

    @pl.when(is_main())
    def _():
        at = 0
        for here, there in zip(mine, others):
            columns = slice(at, at + here.shape[1])
            at += here.shape[1]
            for e in range(2 * part):
                rows = slice(e * per_dev, (e + 1) * per_dev)
                total = (here[rows] + there[rows] + update_ref[rows, columns]).astype(bf16)
                if e < part:
                    near_refs[e][:, columns] = total
                else:
                    far_ref[e - part, :, columns] = total


def split_kernel(far_ref, *out_refs):
    for m, out_ref in enumerate(out_refs):
        out_ref[...] = far_ref[m]


def join_kernel(part, *refs):
    near_refs, far_refs, out_ref = refs[:part], refs[part : 2 * part], refs[2 * part]
    width = near_refs[0].shape[1]
    low = lax.axis_index("adapter") % part

    def put(blocks):
        for m, ref in enumerate(blocks):
            out_ref[:, pl.ds(pl.multiple_of((low ^ m) * width, width), width)] = ref[...]

    main = is_main()

    @pl.when(main)
    def _():
        put(far_refs)

    @pl.when(jnp.logical_not(main))
    def _():
        put(near_refs)


def shards(attended, adapter_index_rows, output_weight, adapter_down_weight, adapter_up_weight):
    per_dev, half_width = attended.shape
    column_width = output_weight.shape[0]
    local, rank_width = adapter_down_weight.shape[:2]
    n = lax.axis_size("adapter")
    cores = lax.axis_size("tensor")
    part = n // cores
    rows = n * per_dev
    both = ("adapter", "tensor")

    def to(source, e, target):
        def core(i, kind):
            return i * cores + (i // part if kind == "side" else 1 - i // part)

        return [(core(i, source), core(i ^ e, target)) for i in range(n)]

    other_up = lax.ppermute(adapter_up_weight, both, to("side", 0, "main"))
    payload = call(
        pack_kernel,
        shape(per_dev, half_width + LANES, dtype=bf16),
        [attended, adapter_index_rows.reshape(1, per_dev)],
        in_hbm=(0, 1),
        flops=AHEAD,
        scratch=[
            pltpu.VMEM((per_dev, half_width), bf16),
            pltpu.VMEM((1, per_dev), i32),
            pltpu.SemaphoreType.DMA((2,)),
        ],
    )
    blocks = [payload] * n
    for e in [*range(2, n, 2), *range(1, n, 2)]:
        if e % 2 == 0:
            blocks[e] = lax.ppermute(payload, "adapter", [(i, i ^ e) for i in range(n)])
        else:
            blocks[e] = lax.ppermute(blocks[e - 1], "adapter", [(i, i ^ 1) for i in range(n)])
    down = adapter_down_weight.reshape(local * rank_width, half_width)
    piece, meta, slots = call(
        functools.partial(shrink_kernel, n, local),
        (
            shape(rows, half_width, dtype=bf16),
            shape(rows, LANES, dtype=i32),
            shape(MOST, local * rank_width),
        ),
        blocks + [other_up, down],
        vmem=16 * MIB,
        in_vmem=(n,),
    )
    wide = local * rank_width
    sections = 1

    def base_part(place, after=()):
        return call(
            functools.partial(base_kernel, place),
            shape(rows, column_width // sections),
            [piece, output_weight, *after],
            vmem=8 * MIB,
            in_vmem=(1,),
            flops=2 * rows * column_width * half_width,
        )

    sums = [
        lax.ppermute(slots, both, to("main", 0, "side")),
        lax.ppermute(slots, both, to("side", part, "side")),
        lax.ppermute(slots, both, to("main", part, "side")),
    ]
    base = [base_part(0)]
    held = call(round_kernel, shape(cores, MOST, wide), [slots, *sums])
    owners = [lax.ppermute(held, both, to("side", e, "main")) for e in range(part)]
    base += [base_part(place, [held]) for place in range(1, sections)]
    other_base = [lax.ppermute(v, both, to("side", 0, "main")) for v in base]
    update = call(
        functools.partial(update_kernel, part, local, rank_width),
        shape(rows, column_width),
        [*owners, meta, adapter_up_weight, other_up],
        vmem=8 * MIB,
        in_vmem=(part + 1, part + 2),
        scratch=[pltpu.VMEM((cores, rows, part * wide), bf16)],
    )
    block = shape(per_dev, column_width, dtype=bf16)
    far, *near = call(
        functools.partial(total_kernel, sections),
        (shape(part, per_dev, column_width, dtype=bf16),) + (block,) * part,
        [*base, *other_base, update],
    )
    far = lax.ppermute(far, both, to("main", part, "side"))
    near = [lax.ppermute(v, both, to("main", e, "side")) for e, v in enumerate(near)]
    far = call(split_kernel, (block,) * part, [far])
    far = [lax.ppermute(v, both, to("side", e, "main")) for e, v in enumerate(far)]
    return call(
        functools.partial(join_kernel, part),
        shape(per_dev, part * column_width, dtype=bf16),
        [*near, *far],
    )


def wide_shards(attended, adapter_index_rows, output_weight, adapter_down_weight, adapter_up_weight):
    per_dev = attended.shape[0]
    column_width = output_weight.shape[0]
    local_count = adapter_down_weight.shape[0]
    rank_width = adapter_down_weight.shape[1]
    owner = lax.axis_index("adapter")
    width_all = lax.axis_size("adapter")
    batch_rows = per_dev * width_all
    all_ids = lax.all_gather(adapter_index_rows, "adapter", axis=0, tiled=True)[:, 0]
    owned = owner * local_count + jnp.arange(local_count, dtype=jnp.int32)
    mine = (all_ids[None, :] == owned[:, None]).astype(jnp.int32)
    order_rank = jnp.cumsum(mine, axis=1) - 1
    slot_numbers = jnp.arange(MOST, dtype=jnp.int32)
    chosen = (mine[:, None, :] == 1) & (order_rank[:, None, :] == slot_numbers[None, :, None])
    chosen_half = chosen.astype(jnp.bfloat16)
    piece = lax.all_gather(attended, "adapter", axis=0, tiled=True)
    product = lax.dot_general(
        piece, output_weight, (((1,), (1,)), ((), ())), preferred_element_type=jnp.float32
    )
    base_portion = product
    selected_rows = jnp.einsum(
        "ksn,nd->ksd", chosen_half, piece, preferred_element_type=jnp.float32
    ).astype(jnp.bfloat16)
    shrink_portion = jnp.einsum(
        "oij,omj->oim", selected_rows, adapter_down_weight, preferred_element_type=jnp.float32
    )
    base_portion, shrink_portion = (base_portion, shrink_portion)
    spread_rows = jnp.einsum(
        "ksn,ksr->nr", chosen.astype(jnp.float32), shrink_portion, precision=lax.Precision.HIGHEST
    )
    shrunk = lax.psum(spread_rows, ("adapter", "tensor")).astype(jnp.bfloat16)
    tensor_place = lax.axis_index("tensor")
    groups_number = adapter_up_weight.shape[1] // rank_width
    shifted = all_ids - tensor_place * groups_number
    block = min(batch_rows, 256)

    def expand(pair):
        ids_block, shrunk_block = pair
        hits = (ids_block[:, None] == jnp.arange(groups_number, dtype=jnp.int32)[None, :]).astype(
            jnp.bfloat16
        )
        expanded_update = (hits[:, :, None] * shrunk_block[:, None, :]).reshape(
            block, groups_number * rank_width
        )
        return lax.dot_general(
            expanded_update,
            adapter_up_weight,
            (((1,), (1,)), ((), ())),
            preferred_element_type=jnp.float32,
        )

    adapter_update = lax.map(
        expand,
        (
            shifted.reshape(batch_rows // block, block),
            shrunk.reshape(batch_rows // block, block, rank_width),
        ),
    )
    running_partial = base_portion + adapter_scale * adapter_update.reshape(
        batch_rows, column_width
    )
    blocks = lax.all_to_all(running_partial, "adapter", split_axis=0, concat_axis=1, tiled=True)
    total = lax.psum_scatter(blocks, "tensor", scatter_dimension=1, tiled=True)
    return total.astype(jnp.bfloat16)


def solution(mesh):
    sizes = mesh.shape
    direct = sizes["adapter"] <= 16 and sizes["tensor"] == 2
    in_specs = (
        P(("groups", "adapter"), "tensor"),
        P(("groups", "adapter"), None),
        P("adapter", "tensor"),
        P("adapter", None, "tensor"),
        P("adapter", "tensor"),
    )
    out_specs = P(("groups", "adapter"), "tensor")
    body = shards if direct else wide_shards
    return jax.shard_map(body, mesh=mesh, in_specs=in_specs, out_specs=out_specs, check_vma=False)
```

```python
import functools

import jax
import jax.numpy as jnp
from jax import lax
from jax.experimental import pallas as pl
from jax.experimental.pallas import tpu as pltpu
from jax.sharding import PartitionSpec as P

MOST = 8
LANES = 128
ID_BASE = 256
AHEAD = 40_000_000_000

adapter_scale = 2.0

f32, bf16, i32 = jnp.float32, jnp.bfloat16, jnp.int32
NT = (((1,), (1,)), ((), ()))
MIB = 1 << 20


def call(body, outs, args, vmem=4 * MIB, scratch=(), in_vmem=(), in_hbm=(), flops=0):
    args = [
        pltpu.with_memory_space_constraint(
            a, pltpu.VMEM if i in in_vmem else pltpu.HBM if i in in_hbm else pl.ANY
        )
        for i, a in enumerate(args)
    ]
    return pl.pallas_call(
        body,
        out_shape=outs,
        in_specs=[
            pl.BlockSpec(memory_space=pltpu.HBM if i in in_hbm else pltpu.VMEM)
            for i in range(len(args))
        ],
        out_specs=jax.tree.map(lambda _: pl.BlockSpec(memory_space=pltpu.VMEM), outs),
        scratch_shapes=list(scratch),
        compiler_params=pltpu.CompilerParams(vmem_limit_bytes=vmem),
        cost_estimate=pl.CostEstimate(flops=flops, bytes_accessed=flops // 100, transcendentals=0)
        if flops
        else None,
    )(*args)


def shape(*dims, dtype=f32):
    return jax.ShapeDtypeStruct(dims, dtype)


def iota(dims, axis):
    return lax.broadcasted_iota(i32, dims, axis)


def pack_kernel(att_hbm, ids_hbm, out_ref, att_ref, ids_ref, sems):
    copies = [
        pltpu.make_async_copy(att_hbm, att_ref, sems.at[0]),
        pltpu.make_async_copy(ids_hbm, ids_ref, sems.at[1]),
    ]
    for c in copies:
        c.start()
    for c in copies:
        c.wait()
    per_dev, width = att_ref.shape
    here = iota((per_dev, per_dev), 0) == iota((per_dev, per_dev), 1)
    ids = jnp.sum(jnp.where(here, ids_ref[...], 0), axis=1, keepdims=True)
    lane = iota((per_dev, LANES), 1)
    digits = jnp.where(lane == 0, ids >> 8, jnp.where(lane == 1, ids & (ID_BASE - 1), 0))
    out_ref[:, :width] = att_ref[...]
    out_ref[:, width:] = digits.astype(f32).astype(bf16)


def shrink_kernel(n, local, *refs):
    blocks, (down_ref, x_ref, meta_ref, slots_ref) = refs[:n], refs[n + 1 :]
    per_dev = blocks[0].shape[0]
    width = x_ref.shape[1]
    rows = n * per_dev
    me = lax.axis_index("adapter")
    whole = jnp.concatenate([b[...].astype(f32) for b in blocks], axis=0)
    x_ref[...] = whole[:, :width].astype(bf16)
    product = lax.dot_general(x_ref[...], down_ref[...], NT, preferred_element_type=f32)
    digits = whole[:, width:]
    lane = iota((rows, LANES), 1)
    ids = jnp.sum(
        jnp.where(lane == 0, digits * ID_BASE, jnp.where(lane == 1, digits, 0.0)),
        axis=1,
        keepdims=True,
    ).astype(i32)
    square = (rows, rows)
    diagonal = iota(square, 0) == iota(square, 1)

    def home(which):
        return ((which // per_dev) ^ me) * per_dev + which % per_dev

    ids_across = jnp.sum(jnp.where(diagonal, ids, 0), axis=0, keepdims=True)
    same = ids == ids_across
    down_order, across_order = home(iota(square, 0)), home(iota(square, 1))
    rank = jnp.sum((same & (across_order < down_order)).astype(i32), axis=1, keepdims=True)
    rank_across = jnp.sum((same & (down_order < across_order)).astype(i32), axis=0, keepdims=True)
    meta_ref[...] = jnp.where(lane == 0, ids, rank)
    rank_width = down_ref.shape[0] // local
    slots = jnp.zeros((MOST, local * rank_width), f32)
    slot_lane = iota(slots.shape, 1)
    for k in range(local):
        picks = (rank_across == iota((MOST, rows), 0)) & (ids_across == me * local + k)
        found = jnp.dot(
            picks.astype(f32), product, precision=lax.Precision.HIGHEST, preferred_element_type=f32
        )
        slots = jnp.where(slot_lane // rank_width == k, found, slots)
    for j in range(slots_ref.shape[0]):
        slots_ref[j] = slots


def base_kernel(x_ref, weight_ref, out_ref):
    out_ref[0] = lax.dot_general(x_ref[...], weight_ref[...], NT, preferred_element_type=f32)


def base_call(x, weight, cores, steps):
    rows, depth = x.shape
    width = weight.shape[0] // steps
    each = steps // cores
    return pl.pallas_call(
        base_kernel,
        grid=(steps,),
        out_shape=shape(cores, rows, each * width),
        in_specs=[
            pl.BlockSpec((rows, depth), lambda i: (0, 0)),
            pl.BlockSpec((width, depth), lambda i: (i, 0)),
        ],
        out_specs=pl.BlockSpec((1, rows, width), lambda i: (i // each, 0, i % each)),
        compiler_params=pltpu.CompilerParams(vmem_limit_bytes=16 * MIB),
        cost_estimate=pl.CostEstimate(
            flops=2 * rows * steps * width * depth,
            bytes_accessed=2 * steps * width * depth,
            transcendentals=0,
        ),
    )(x, pltpu.with_memory_space_constraint(weight, pltpu.HBM))


def update_kernel(n, cores, local, rank_width, *refs):
    meta_ref, slots_ref, up_ref, other_up_ref, out_ref, spread_ref = refs
    part = n // cores
    rows, width = out_ref.shape
    core = lax.axis_index("tensor")
    ids, rank = meta_ref[:, :1], meta_ref[:, 1:2]
    picks = (rank == iota((rows, MOST), 1)).astype(f32).astype(bf16)
    for half in range(cores):
        owners = [
            sum(slots_ref[a * cores + t] for t in range(1, cores)) + slots_ref[a * cores]
            for a in range(half * part, (half + 1) * part)
        ]
        table = jnp.concatenate(owners, axis=1).astype(bf16)
        spread = jnp.dot(picks, table, preferred_element_type=f32)
        wanted = iota(spread.shape, 1) // rank_width + half * part * local
        spread_ref[half] = jnp.where(ids == wanted, spread, 0.0).astype(bf16)
    mine = pl.ds(pl.multiple_of(core * width, width), width)
    update = lax.dot_general(spread_ref[core], up_ref[mine, :], NT, preferred_element_type=f32)
    update += lax.dot_general(
        spread_ref[1 - core], other_up_ref[mine, :], NT, preferred_element_type=f32
    )
    out_ref[...] = adapter_scale * update


def total_kernel(cores, base_ref, other_ref, update_ref, out_ref):
    per_dev = out_ref.shape[1]
    me, core = lax.axis_index("adapter"), lax.axis_index("tensor")
    total = (base_ref[core] + other_ref[core] + update_ref[...]).astype(bf16)
    for e in range(out_ref.shape[0] // cores):
        for t in range(cores):
            out_ref[(me ^ e) * cores + t] = total[e * per_dev : (e + 1) * per_dev]


def join_kernel(cores, blocks_ref, out_ref):
    count = blocks_ref.shape[0] // cores
    width = blocks_ref.shape[2]
    first = lax.axis_index("tensor") * count
    for j in range(count):
        out_ref[:, j * width : (j + 1) * width] = blocks_ref[first + j]


def shards(attended, adapter_index_rows, output_weight, adapter_down_weight, adapter_up_weight):
    per_dev, half_width = attended.shape
    column_width = output_weight.shape[0]
    local, rank_width = adapter_down_weight.shape[:2]
    n = lax.axis_size("adapter")
    cores = lax.axis_size("tensor")
    part = n // cores
    rows = n * per_dev
    both = ("adapter", "tensor")

    swap = [(i * cores + t, i * cores + 1 - t) for i in range(n) for t in range(cores)]
    other_up = lax.ppermute(adapter_up_weight, both, swap)
    payload = call(
        pack_kernel,
        shape(per_dev, half_width + LANES, dtype=bf16),
        [attended, adapter_index_rows.reshape(1, per_dev)],
        in_hbm=(0, 1),
        flops=AHEAD,
        scratch=[
            pltpu.VMEM((per_dev, half_width), bf16),
            pltpu.VMEM((1, per_dev), i32),
            pltpu.SemaphoreType.DMA((2,)),
        ],
    )
    blocks = [payload] * n
    for e in [*range(2, n, 2), *range(1, n, 2)]:
        if e % 2 == 0:
            blocks[e] = lax.ppermute(payload, "adapter", [(i, i ^ e) for i in range(n)])
        else:
            blocks[e] = lax.ppermute(blocks[e - 1], "adapter", [(i, i ^ 1) for i in range(n)])
    down = adapter_down_weight.reshape(local * rank_width, half_width)
    piece, meta, slots = call(
        functools.partial(shrink_kernel, n, local),
        (
            shape(rows, half_width, dtype=bf16),
            shape(rows, LANES, dtype=i32),
            shape(n * cores, MOST, local * rank_width),
        ),
        blocks + [other_up, down],
        vmem=16 * MIB,
        in_vmem=(n,),
    )
    wide = local * rank_width
    kept = column_width // cores
    slots = lax.all_to_all(slots, both, split_axis=0, concat_axis=0, tiled=True)
    base = base_call(piece, output_weight, cores, 8)
    other = lax.ppermute(base, both, swap)
    update = call(
        functools.partial(update_kernel, n, cores, local, rank_width),
        shape(rows, kept),
        [meta, slots, adapter_up_weight, other_up],
        vmem=8 * MIB,
        in_vmem=(2, 3),
        scratch=[pltpu.VMEM((cores, rows, part * wide), bf16)],
    )
    total = call(
        functools.partial(total_kernel, cores),
        shape(n * cores, per_dev, kept, dtype=bf16),
        [base, other, update],
    )
    blocks = lax.all_to_all(total, both, split_axis=0, concat_axis=0, tiled=True)
    return call(
        functools.partial(join_kernel, cores),
        shape(per_dev, part * column_width, dtype=bf16),
        [blocks],
    )


def wide_shards(attended, adapter_index_rows, output_weight, adapter_down_weight, adapter_up_weight):
    per_dev = attended.shape[0]
    column_width = output_weight.shape[0]
    local_count = adapter_down_weight.shape[0]
    rank_width = adapter_down_weight.shape[1]
    owner = lax.axis_index("adapter")
    width_all = lax.axis_size("adapter")
    batch_rows = per_dev * width_all
    all_ids = lax.all_gather(adapter_index_rows, "adapter", axis=0, tiled=True)[:, 0]
    owned = owner * local_count + jnp.arange(local_count, dtype=jnp.int32)
    mine = (all_ids[None, :] == owned[:, None]).astype(jnp.int32)
    order_rank = jnp.cumsum(mine, axis=1) - 1
    slot_numbers = jnp.arange(MOST, dtype=jnp.int32)
    chosen = (mine[:, None, :] == 1) & (order_rank[:, None, :] == slot_numbers[None, :, None])
    chosen_half = chosen.astype(jnp.bfloat16)
    piece = lax.all_gather(attended, "adapter", axis=0, tiled=True)
    product = lax.dot_general(
        piece, output_weight, (((1,), (1,)), ((), ())), preferred_element_type=jnp.float32
    )
    base_portion = product
    selected_rows = jnp.einsum(
        "ksn,nd->ksd", chosen_half, piece, preferred_element_type=jnp.float32
    ).astype(jnp.bfloat16)
    shrink_portion = jnp.einsum(
        "oij,omj->oim", selected_rows, adapter_down_weight, preferred_element_type=jnp.float32
    )
    base_portion, shrink_portion = (base_portion, shrink_portion)
    spread_rows = jnp.einsum(
        "ksn,ksr->nr", chosen.astype(jnp.float32), shrink_portion, precision=lax.Precision.HIGHEST
    )
    shrunk = lax.psum(spread_rows, ("adapter", "tensor")).astype(jnp.bfloat16)
    tensor_place = lax.axis_index("tensor")
    groups_number = adapter_up_weight.shape[1] // rank_width
    shifted = all_ids - tensor_place * groups_number
    block = min(batch_rows, 256)

    def expand(pair):
        ids_block, shrunk_block = pair
        hits = (ids_block[:, None] == jnp.arange(groups_number, dtype=jnp.int32)[None, :]).astype(
            jnp.bfloat16
        )
        expanded_update = (hits[:, :, None] * shrunk_block[:, None, :]).reshape(
            block, groups_number * rank_width
        )
        return lax.dot_general(
            expanded_update,
            adapter_up_weight,
            (((1,), (1,)), ((), ())),
            preferred_element_type=jnp.float32,
        )

    adapter_update = lax.map(
        expand,
        (
            shifted.reshape(batch_rows // block, block),
            shrunk.reshape(batch_rows // block, block, rank_width),
        ),
    )
    running_partial = base_portion + adapter_scale * adapter_update.reshape(
        batch_rows, column_width
    )
    blocks = lax.all_to_all(running_partial, "adapter", split_axis=0, concat_axis=1, tiled=True)
    total = lax.psum_scatter(blocks, "tensor", scatter_dimension=1, tiled=True)
    return total.astype(jnp.bfloat16)


def solution(mesh):
    sizes = mesh.shape
    direct = sizes["adapter"] <= 16 and sizes["tensor"] == 2
    in_specs = (
        P(("groups", "adapter"), "tensor"),
        P(("groups", "adapter"), None),
        P("adapter", "tensor"),
        P("adapter", None, "tensor"),
        P("adapter", "tensor"),
    )
    out_specs = P(("groups", "adapter"), "tensor")
    body = shards if direct else wide_shards
    return jax.shard_map(body, mesh=mesh, in_specs=in_specs, out_specs=out_specs, check_vma=False)
```

```python
import functools

import jax
import jax.numpy as jnp
from jax import lax
from jax.experimental import pallas as pl
from jax.experimental.pallas import tpu as pltpu
from jax.sharding import PartitionSpec as P

MOST = 8
LANES = 128
ID_BASE = 256
AHEAD = 40_000_000_000

adapter_scale = 2.0

f32, bf16, i32 = jnp.float32, jnp.bfloat16, jnp.int32
NT = (((1,), (1,)), ((), ()))
MIB = 1 << 20


def call(body, outs, args, vmem=4 * MIB, scratch=(), in_vmem=(), in_hbm=(), flops=0):
    args = [
        pltpu.with_memory_space_constraint(
            a, pltpu.VMEM if i in in_vmem else pltpu.HBM if i in in_hbm else pl.ANY
        )
        for i, a in enumerate(args)
    ]
    return pl.pallas_call(
        body,
        out_shape=outs,
        in_specs=[
            pl.BlockSpec(memory_space=pltpu.HBM if i in in_hbm else pltpu.VMEM)
            for i in range(len(args))
        ],
        out_specs=jax.tree.map(lambda _: pl.BlockSpec(memory_space=pltpu.VMEM), outs),
        scratch_shapes=list(scratch),
        compiler_params=pltpu.CompilerParams(vmem_limit_bytes=vmem),
        cost_estimate=pl.CostEstimate(flops=flops, bytes_accessed=flops // 100, transcendentals=0)
        if flops
        else None,
    )(*args)


def shape(*dims, dtype=f32):
    return jax.ShapeDtypeStruct(dims, dtype)


def iota(dims, axis):
    return lax.broadcasted_iota(i32, dims, axis)


def pack_kernel(att_hbm, ids_hbm, out_ref, att_ref, ids_ref, sems):
    copies = [
        pltpu.make_async_copy(att_hbm, att_ref, sems.at[0]),
        pltpu.make_async_copy(ids_hbm, ids_ref, sems.at[1]),
    ]
    for c in copies:
        c.start()
    for c in copies:
        c.wait()
    per_dev, width = att_ref.shape
    here = iota((per_dev, per_dev), 0) == iota((per_dev, per_dev), 1)
    ids = jnp.sum(jnp.where(here, ids_ref[...], 0), axis=1, keepdims=True)
    lane = iota((per_dev, LANES), 1)
    digits = jnp.where(lane == 0, ids >> 8, jnp.where(lane == 1, ids & (ID_BASE - 1), 0))
    out_ref[:, :width] = att_ref[...]
    out_ref[:, width:] = digits.astype(f32).astype(bf16)


def shrink_kernel(n, local, *refs):
    blocks, (down_ref, x_ref, meta_ref, slots_ref) = refs[:n], refs[n + 1 :]
    per_dev = blocks[0].shape[0]
    width = x_ref.shape[1]
    rows = n * per_dev
    me = lax.axis_index("adapter")
    whole = jnp.concatenate([b[...].astype(f32) for b in blocks], axis=0)
    x_ref[...] = whole[:, :width].astype(bf16)
    product = lax.dot_general(x_ref[...], down_ref[...], NT, preferred_element_type=f32)
    digits = whole[:, width:]
    lane = iota((rows, LANES), 1)
    ids = jnp.sum(
        jnp.where(lane == 0, digits * ID_BASE, jnp.where(lane == 1, digits, 0.0)),
        axis=1,
        keepdims=True,
    ).astype(i32)
    square = (rows, rows)
    diagonal = iota(square, 0) == iota(square, 1)

    def home(which):
        return ((which // per_dev) ^ me) * per_dev + which % per_dev

    ids_across = jnp.sum(jnp.where(diagonal, ids, 0), axis=0, keepdims=True)
    same = ids == ids_across
    down_order, across_order = home(iota(square, 0)), home(iota(square, 1))
    rank = jnp.sum((same & (across_order < down_order)).astype(i32), axis=1, keepdims=True)
    rank_across = jnp.sum((same & (down_order < across_order)).astype(i32), axis=0, keepdims=True)
    meta_ref[...] = jnp.where(lane == 0, ids, rank)
    rank_width = down_ref.shape[0] // local
    slots = jnp.zeros((MOST, local * rank_width), f32)
    slot_lane = iota(slots.shape, 1)
    for k in range(local):
        picks = (rank_across == iota((MOST, rows), 0)) & (ids_across == me * local + k)
        found = jnp.dot(
            picks.astype(f32), product, precision=lax.Precision.HIGHEST, preferred_element_type=f32
        )
        slots = jnp.where(slot_lane // rank_width == k, found, slots)
    slots_ref[...] = slots


def base_kernel(place, x_ref, weight_ref, *refs):
    out_ref = refs[-1]
    width = out_ref.shape[1]
    out_ref[...] = lax.dot_general(
        x_ref[...],
        weight_ref[place * width : (place + 1) * width, :],
        NT,
        preferred_element_type=f32,
    )


def round_kernel(mine_ref, other_ref, across_ref, across_other_ref, *refs):
    out_ref = refs[-1]
    out_ref[0] = (mine_ref[...] + other_ref[...]).astype(bf16).astype(f32)
    out_ref[1] = (across_ref[...] + across_other_ref[...]).astype(bf16).astype(f32)


def near_place():
    part = lax.axis_size("adapter") // lax.axis_size("tensor")
    return lax.axis_index("tensor") == lax.axis_index("adapter") // part


def kept_rows(count, near):
    keep = jnp.where(near, 0, count)
    return pl.ds(pl.multiple_of(keep, count), count), pl.ds(
        pl.multiple_of(count - keep, count), count
    )


def split_kernel(*refs):
    parts, (keep_ref, give_ref) = refs[:-2], refs[-2:]
    keep, give = kept_rows(keep_ref.shape[0], near_place())
    at = 0
    for part in parts:
        columns = slice(at, at + part.shape[1])
        keep_ref[:, columns] = part[keep, :]
        give_ref[:, columns] = part[give, :]
        at += part.shape[1]


def update_kernel(part, local, rank_width, *refs):
    owners = refs[:part]
    meta_ref, up_ref, other_up_ref, out_ref, spread_ref = refs[part:]
    rows = out_ref.shape[0]
    me, core = lax.axis_index("adapter"), lax.axis_index("tensor")
    keep, _ = kept_rows(rows, near_place())
    meta = meta_ref[keep, :]
    ids, rank = meta[:, :1], meta[:, 1:2]
    picks = (rank == iota((rows, MOST), 1)).astype(f32).astype(bf16)
    wide = local * rank_width
    for e, slots_ref in enumerate(owners):
        for across in range(slots_ref.shape[0]):
            owner = me ^ (e + across * part)
            spread = jnp.dot(picks, slots_ref[across].astype(bf16), preferred_element_type=f32)
            wanted = iota(spread.shape, 1) // rank_width + owner * local
            at = pl.ds(pl.multiple_of(owner % part * wide, wide), wide)
            spread = jnp.where(ids == wanted, spread, 0.0).astype(bf16)
            spread_ref[owner // part, :, at] = spread
    update = lax.dot_general(spread_ref[core], up_ref[...], NT, preferred_element_type=f32)
    update += lax.dot_general(
        spread_ref[1 - core], other_up_ref[...], NT, preferred_element_type=f32
    )
    out_ref[...] = adapter_scale * update


def total_kernel(keep_ref, other_ref, update_ref, out_ref):
    per_dev = out_ref.shape[1]
    for e in range(out_ref.shape[0]):
        at = slice(e * per_dev, (e + 1) * per_dev)
        out_ref[e] = (keep_ref[at] + other_ref[at] + update_ref[at]).astype(bf16)


def unstack_kernel(stacked_ref, *out_refs):
    for m, out_ref in enumerate(out_refs):
        out_ref[...] = stacked_ref[m]


def join_kernel(*refs):
    blocks, out_ref = refs[:-1], refs[-1]
    part, width = len(blocks), blocks[0].shape[1]
    low = lax.axis_index("adapter") % part
    for m, ref in enumerate(blocks):
        out_ref[:, pl.ds(pl.multiple_of((low ^ m) * width, width), width)] = ref[...]


def shards(attended, adapter_index_rows, output_weight, adapter_down_weight, adapter_up_weight):
    per_dev, half_width = attended.shape
    column_width = output_weight.shape[0]
    local, rank_width = adapter_down_weight.shape[:2]
    n = lax.axis_size("adapter")
    cores = lax.axis_size("tensor")
    part = n // cores
    rows = n * per_dev
    both = ("adapter", "tensor")

    def to(e, other):
        return [(i * cores + t, (i ^ e) * cores + (t ^ other)) for i in range(n) for t in range(cores)]

    other_up = lax.ppermute(adapter_up_weight, both, to(0, 1))
    payload = call(
        pack_kernel,
        shape(per_dev, half_width + LANES, dtype=bf16),
        [attended, adapter_index_rows.reshape(1, per_dev)],
        in_hbm=(0, 1),
        flops=AHEAD,
        scratch=[
            pltpu.VMEM((per_dev, half_width), bf16),
            pltpu.VMEM((1, per_dev), i32),
            pltpu.SemaphoreType.DMA((2,)),
        ],
    )
    blocks = [payload] * n
    for e in [*range(2, n, 2), *range(1, n, 2)]:
        if e % 2 == 0:
            blocks[e] = lax.ppermute(payload, "adapter", [(i, i ^ e) for i in range(n)])
        else:
            blocks[e] = lax.ppermute(blocks[e - 1], "adapter", [(i, i ^ 1) for i in range(n)])
    down = adapter_down_weight.reshape(local * rank_width, half_width)
    piece, meta, slots = call(
        functools.partial(shrink_kernel, n, local),
        (
            shape(rows, half_width, dtype=bf16),
            shape(rows, LANES, dtype=i32),
            shape(MOST, local * rank_width),
        ),
        blocks + [other_up, down],
        vmem=16 * MIB,
        in_vmem=(n,),
    )
    sections = 1

    def base_part(place, after=()):
        return call(
            functools.partial(base_kernel, place),
            shape(rows, column_width // sections),
            [piece, output_weight, *after],
            vmem=8 * MIB,
            in_vmem=(1,),
            flops=rows * column_width * half_width,
        )

    wide = local * rank_width
    sums = [
        lax.ppermute(slots, both, to(0, 1)),
        lax.ppermute(slots, both, to(part, 0)),
        lax.ppermute(slots, both, to(part, 1)),
    ]
    base = [base_part(0, sums[:1])]
    held = call(round_kernel, shape(cores, MOST, wide), [slots, *sums, *base])
    owners = [held] + [lax.ppermute(held, both, to(e, 0)) for e in range(1, part)]
    base += [base_part(place, owners[1:2]) for place in range(1, sections)]
    kept = shape(rows // cores, column_width)
    keep, give = call(split_kernel, (kept, kept), base)
    other = lax.ppermute(give, both, to(0, 1))
    update = call(
        functools.partial(update_kernel, part, local, rank_width),
        kept,
        [*owners, meta, adapter_up_weight, other_up],
        vmem=8 * MIB,
        in_vmem=(part + 1, part + 2),
        flops=4_000_000_000,
        scratch=[pltpu.VMEM((cores, rows // cores, part * wide), bf16)],
    )
    total = call(
        total_kernel, shape(part, per_dev, column_width, dtype=bf16), [keep, other, update]
    )
    pairs = []
    for i in range(n):
        half = i // part
        pairs.append((i * cores + half, i * cores + half))
        pairs.append((i * cores + 1 - half, (i ^ part) * cores + half))
    total = lax.ppermute(total, both, pairs)
    block = shape(per_dev, column_width, dtype=bf16)
    blocks = call(unstack_kernel, (block,) * part, [total])
    blocks = [v if m == 0 else lax.ppermute(v, both, to(m, 0)) for m, v in enumerate(blocks)]
    return call(join_kernel, shape(per_dev, part * column_width, dtype=bf16), blocks)


def wide_shards(attended, adapter_index_rows, output_weight, adapter_down_weight, adapter_up_weight):
    per_dev = attended.shape[0]
    column_width = output_weight.shape[0]
    local_count = adapter_down_weight.shape[0]
    rank_width = adapter_down_weight.shape[1]
    owner = lax.axis_index("adapter")
    width_all = lax.axis_size("adapter")
    batch_rows = per_dev * width_all
    all_ids = lax.all_gather(adapter_index_rows, "adapter", axis=0, tiled=True)[:, 0]
    owned = owner * local_count + jnp.arange(local_count, dtype=jnp.int32)
    mine = (all_ids[None, :] == owned[:, None]).astype(jnp.int32)
    order_rank = jnp.cumsum(mine, axis=1) - 1
    slot_numbers = jnp.arange(MOST, dtype=jnp.int32)
    chosen = (mine[:, None, :] == 1) & (order_rank[:, None, :] == slot_numbers[None, :, None])
    chosen_half = chosen.astype(jnp.bfloat16)
    piece = lax.all_gather(attended, "adapter", axis=0, tiled=True)
    product = lax.dot_general(
        piece, output_weight, (((1,), (1,)), ((), ())), preferred_element_type=jnp.float32
    )
    base_portion = product
    selected_rows = jnp.einsum(
        "ksn,nd->ksd", chosen_half, piece, preferred_element_type=jnp.float32
    ).astype(jnp.bfloat16)
    shrink_portion = jnp.einsum(
        "oij,omj->oim", selected_rows, adapter_down_weight, preferred_element_type=jnp.float32
    )
    base_portion, shrink_portion = (base_portion, shrink_portion)
    spread_rows = jnp.einsum(
        "ksn,ksr->nr", chosen.astype(jnp.float32), shrink_portion, precision=lax.Precision.HIGHEST
    )
    shrunk = lax.psum(spread_rows, ("adapter", "tensor")).astype(jnp.bfloat16)
    tensor_place = lax.axis_index("tensor")
    groups_number = adapter_up_weight.shape[1] // rank_width
    shifted = all_ids - tensor_place * groups_number
    block = min(batch_rows, 256)

    def expand(pair):
        ids_block, shrunk_block = pair
        hits = (ids_block[:, None] == jnp.arange(groups_number, dtype=jnp.int32)[None, :]).astype(
            jnp.bfloat16
        )
        expanded_update = (hits[:, :, None] * shrunk_block[:, None, :]).reshape(
            block, groups_number * rank_width
        )
        return lax.dot_general(
            expanded_update,
            adapter_up_weight,
            (((1,), (1,)), ((), ())),
            preferred_element_type=jnp.float32,
        )

    adapter_update = lax.map(
        expand,
        (
            shifted.reshape(batch_rows // block, block),
            shrunk.reshape(batch_rows // block, block, rank_width),
        ),
    )
    running_partial = base_portion + adapter_scale * adapter_update.reshape(
        batch_rows, column_width
    )
    blocks = lax.all_to_all(running_partial, "adapter", split_axis=0, concat_axis=1, tiled=True)
    total = lax.psum_scatter(blocks, "tensor", scatter_dimension=1, tiled=True)
    return total.astype(jnp.bfloat16)


def solution(mesh):
    sizes = mesh.shape
    direct = sizes["adapter"] <= 16 and sizes["tensor"] == 2
    in_specs = (
        P(("groups", "adapter"), "tensor"),
        P(("groups", "adapter"), None),
        P("adapter", "tensor"),
        P("adapter", None, "tensor"),
        P("adapter", "tensor"),
    )
    out_specs = P(("groups", "adapter"), "tensor")
    body = shards if direct else wide_shards
    return jax.shard_map(body, mesh=mesh, in_specs=in_specs, out_specs=out_specs, check_vma=False)
```

```python
import functools

import jax
import jax.numpy as jnp
from jax import lax
from jax.experimental import pallas as pl
from jax.experimental.pallas import tpu as pltpu
from jax.sharding import PartitionSpec as P

MOST = 8
LANES = 128
ID_BASE = 256
AHEAD = 40_000_000_000

adapter_scale = 2.0

f32, bf16, i32 = jnp.float32, jnp.bfloat16, jnp.int32
NT = (((1,), (1,)), ((), ()))
MIB = 1 << 20


def call(body, outs, args, vmem=4 * MIB, scratch=(), in_vmem=(), in_hbm=(), flops=0):
    args = [
        pltpu.with_memory_space_constraint(
            a, pltpu.VMEM if i in in_vmem else pltpu.HBM if i in in_hbm else pl.ANY
        )
        for i, a in enumerate(args)
    ]
    return pl.pallas_call(
        body,
        out_shape=outs,
        in_specs=[
            pl.BlockSpec(memory_space=pltpu.HBM if i in in_hbm else pltpu.VMEM)
            for i in range(len(args))
        ],
        out_specs=jax.tree.map(lambda _: pl.BlockSpec(memory_space=pltpu.VMEM), outs),
        scratch_shapes=list(scratch),
        compiler_params=pltpu.CompilerParams(vmem_limit_bytes=vmem),
        cost_estimate=pl.CostEstimate(flops=flops, bytes_accessed=flops // 100, transcendentals=0)
        if flops
        else None,
    )(*args)


def shape(*dims, dtype=f32):
    return jax.ShapeDtypeStruct(dims, dtype)


def iota(dims, axis):
    return lax.broadcasted_iota(i32, dims, axis)


def pack_kernel(att_hbm, ids_hbm, out_ref, att_ref, ids_ref, sems):
    copies = [
        pltpu.make_async_copy(att_hbm, att_ref, sems.at[0]),
        pltpu.make_async_copy(ids_hbm, ids_ref, sems.at[1]),
    ]
    for c in copies:
        c.start()
    for c in copies:
        c.wait()
    per_dev, width = att_ref.shape
    here = iota((per_dev, per_dev), 0) == iota((per_dev, per_dev), 1)
    ids = jnp.sum(jnp.where(here, ids_ref[...], 0), axis=1, keepdims=True)
    lane = iota((per_dev, LANES), 1)
    digits = jnp.where(lane == 0, ids >> 8, jnp.where(lane == 1, ids & (ID_BASE - 1), 0))
    out_ref[:, :width] = att_ref[...]
    out_ref[:, width:] = digits.astype(f32).astype(bf16)


def shrink_kernel(n, local, *refs):
    blocks, (down_ref, x_ref, meta_ref, slots_ref) = refs[:n], refs[n + 1 :]
    per_dev = blocks[0].shape[0]
    width = x_ref.shape[1]
    rows = n * per_dev
    me = lax.axis_index("adapter")
    whole = jnp.concatenate([b[...].astype(f32) for b in blocks], axis=0)
    x_ref[...] = whole[:, :width].astype(bf16)
    product = lax.dot_general(x_ref[...], down_ref[...], NT, preferred_element_type=f32)
    digits = whole[:, width:]
    lane = iota((rows, LANES), 1)
    ids = jnp.sum(
        jnp.where(lane == 0, digits * ID_BASE, jnp.where(lane == 1, digits, 0.0)),
        axis=1,
        keepdims=True,
    ).astype(i32)
    square = (rows, rows)
    diagonal = iota(square, 0) == iota(square, 1)

    def home(which):
        return ((which // per_dev) ^ me) * per_dev + which % per_dev

    ids_across = jnp.sum(jnp.where(diagonal, ids, 0), axis=0, keepdims=True)
    same = ids == ids_across
    down_order, across_order = home(iota(square, 0)), home(iota(square, 1))
    rank = jnp.sum((same & (across_order < down_order)).astype(i32), axis=1, keepdims=True)
    rank_across = jnp.sum((same & (down_order < across_order)).astype(i32), axis=0, keepdims=True)
    meta_ref[...] = jnp.where(lane == 0, ids, rank)
    rank_width = down_ref.shape[0] // local
    slots = jnp.zeros((MOST, local * rank_width), f32)
    slot_lane = iota(slots.shape, 1)
    for k in range(local):
        picks = (rank_across == iota((MOST, rows), 0)) & (ids_across == me * local + k)
        found = jnp.dot(
            picks.astype(f32), product, precision=lax.Precision.HIGHEST, preferred_element_type=f32
        )
        slots = jnp.where(slot_lane // rank_width == k, found, slots)
    slots_ref[...] = slots


def base_kernel(place, x_ref, weight_ref, *refs):
    out_ref = refs[-1]
    width = out_ref.shape[1]
    out_ref[...] = lax.dot_general(
        x_ref[...],
        weight_ref[place * width : (place + 1) * width, :],
        NT,
        preferred_element_type=f32,
    )


def round_kernel(mine_ref, other_ref, across_ref, across_other_ref, *refs):
    out_ref = refs[-1]
    out_ref[0] = (mine_ref[...] + other_ref[...]).astype(bf16).astype(f32)
    out_ref[1] = (across_ref[...] + across_other_ref[...]).astype(bf16).astype(f32)


def near_place():
    part = lax.axis_size("adapter") // lax.axis_size("tensor")
    return lax.axis_index("tensor") == lax.axis_index("adapter") // part


def kept_rows(count, near):
    keep = jnp.where(near, 0, count)
    return pl.ds(pl.multiple_of(keep, count), count), pl.ds(
        pl.multiple_of(count - keep, count), count
    )


def split_kernel(*refs):
    parts, (keep_ref, give_ref) = refs[:-2], refs[-2:]
    keep, give = kept_rows(keep_ref.shape[0], near_place())
    at = 0
    for part in parts:
        columns = slice(at, at + part.shape[1])
        keep_ref[:, columns] = part[keep, :]
        give_ref[:, columns] = part[give, :]
        at += part.shape[1]


def update_kernel(part, local, rank_width, *refs):
    owners = refs[:part]
    meta_ref, up_ref, other_up_ref, out_ref, spread_ref = refs[part:]
    rows = out_ref.shape[0]
    me, core = lax.axis_index("adapter"), lax.axis_index("tensor")
    keep, _ = kept_rows(rows, near_place())
    meta = meta_ref[keep, :]
    ids, rank = meta[:, :1], meta[:, 1:2]
    picks = (rank == iota((rows, MOST), 1)).astype(f32).astype(bf16)
    wide = local * rank_width
    for e, slots_ref in enumerate(owners):
        for across in range(slots_ref.shape[0]):
            owner = me ^ (e + across * part)
            spread = jnp.dot(picks, slots_ref[across].astype(bf16), preferred_element_type=f32)
            wanted = iota(spread.shape, 1) // rank_width + owner * local
            at = pl.ds(pl.multiple_of(owner % part * wide, wide), wide)
            spread = jnp.where(ids == wanted, spread, 0.0).astype(bf16)
            spread_ref[owner // part, :, at] = spread
    update = lax.dot_general(spread_ref[core], up_ref[...], NT, preferred_element_type=f32)
    update += lax.dot_general(
        spread_ref[1 - core], other_up_ref[...], NT, preferred_element_type=f32
    )
    out_ref[...] = adapter_scale * update


def total_kernel(keep_ref, other_ref, update_ref, out_ref):
    per_dev = out_ref.shape[1]
    for e in range(out_ref.shape[0]):
        at = slice(e * per_dev, (e + 1) * per_dev)
        out_ref[e] = (keep_ref[at] + other_ref[at] + update_ref[at]).astype(bf16)


def unstack_kernel(mine_ref, across_ref, *out_refs):
    near = near_place()
    for m, out_ref in enumerate(out_refs):
        out_ref[...] = jnp.where(near, mine_ref[m].astype(f32), across_ref[m].astype(f32)).astype(
            bf16
        )


def join_kernel(*refs):
    blocks, out_ref = refs[:-1], refs[-1]
    part, width = len(blocks), blocks[0].shape[1]
    low = lax.axis_index("adapter") % part
    for m, ref in enumerate(blocks):
        out_ref[:, pl.ds(pl.multiple_of((low ^ m) * width, width), width)] = ref[...]


def shards(attended, adapter_index_rows, output_weight, adapter_down_weight, adapter_up_weight):
    per_dev, half_width = attended.shape
    column_width = output_weight.shape[0]
    local, rank_width = adapter_down_weight.shape[:2]
    n = lax.axis_size("adapter")
    cores = lax.axis_size("tensor")
    part = n // cores
    rows = n * per_dev
    both = ("adapter", "tensor")

    def to(e, other):
        return [(i * cores + t, (i ^ e) * cores + (t ^ other)) for i in range(n) for t in range(cores)]

    other_up = lax.ppermute(adapter_up_weight, both, to(0, 1))
    payload = call(
        pack_kernel,
        shape(per_dev, half_width + LANES, dtype=bf16),
        [attended, adapter_index_rows.reshape(1, per_dev)],
        in_hbm=(0, 1),
        flops=AHEAD,
        scratch=[
            pltpu.VMEM((per_dev, half_width), bf16),
            pltpu.VMEM((1, per_dev), i32),
            pltpu.SemaphoreType.DMA((2,)),
        ],
    )
    blocks = [payload] * n
    for e in [*range(2, n, 2), *range(1, n, 2)]:
        if e % 2 == 0:
            blocks[e] = lax.ppermute(payload, "adapter", [(i, i ^ e) for i in range(n)])
        else:
            blocks[e] = lax.ppermute(blocks[e - 1], "adapter", [(i, i ^ 1) for i in range(n)])
    down = adapter_down_weight.reshape(local * rank_width, half_width)
    piece, meta, slots = call(
        functools.partial(shrink_kernel, n, local),
        (
            shape(rows, half_width, dtype=bf16),
            shape(rows, LANES, dtype=i32),
            shape(MOST, local * rank_width),
        ),
        blocks + [other_up, down],
        vmem=16 * MIB,
        in_vmem=(n,),
    )
    sections = 2

    def base_part(place, after=()):
        return call(
            functools.partial(base_kernel, place),
            shape(rows, column_width // sections),
            [piece, output_weight, *after],
            vmem=8 * MIB,
            in_vmem=(1,),
            flops=rows * column_width * half_width,
        )

    wide = local * rank_width
    sums = [
        lax.ppermute(slots, both, to(0, 1)),
        lax.ppermute(slots, both, to(part, 0)),
        lax.ppermute(slots, both, to(part, 1)),
    ]
    base = [base_part(0, sums[:1])]
    held = call(round_kernel, shape(cores, MOST, wide), [slots, *sums, *base])
    owners = [held] + [lax.ppermute(held, both, to(e, 0)) for e in range(1, part)]
    base += [base_part(place, owners[-1:]) for place in range(1, sections)]
    kept = shape(rows // cores, column_width)
    keep, give = call(split_kernel, (kept, kept), base)
    other = lax.ppermute(give, both, to(0, 1))
    update = call(
        functools.partial(update_kernel, part, local, rank_width),
        kept,
        [*owners, meta, adapter_up_weight, other_up],
        vmem=8 * MIB,
        in_vmem=(part + 1, part + 2),
        flops=4_000_000_000,
        scratch=[pltpu.VMEM((cores, rows // cores, part * wide), bf16)],
    )
    total = call(
        total_kernel, shape(part, per_dev, column_width, dtype=bf16), [keep, other, update]
    )
    across = lax.ppermute(total, both, to(part, 1))
    block = shape(per_dev, column_width, dtype=bf16)
    blocks = call(unstack_kernel, (block,) * part, [total, across])
    blocks = [v if m == 0 else lax.ppermute(v, both, to(m, 0)) for m, v in enumerate(blocks)]
    return call(join_kernel, shape(per_dev, part * column_width, dtype=bf16), blocks)


def wide_shards(attended, adapter_index_rows, output_weight, adapter_down_weight, adapter_up_weight):
    per_dev = attended.shape[0]
    column_width = output_weight.shape[0]
    local_count = adapter_down_weight.shape[0]
    rank_width = adapter_down_weight.shape[1]
    owner = lax.axis_index("adapter")
    width_all = lax.axis_size("adapter")
    batch_rows = per_dev * width_all
    all_ids = lax.all_gather(adapter_index_rows, "adapter", axis=0, tiled=True)[:, 0]
    owned = owner * local_count + jnp.arange(local_count, dtype=jnp.int32)
    mine = (all_ids[None, :] == owned[:, None]).astype(jnp.int32)
    order_rank = jnp.cumsum(mine, axis=1) - 1
    slot_numbers = jnp.arange(MOST, dtype=jnp.int32)
    chosen = (mine[:, None, :] == 1) & (order_rank[:, None, :] == slot_numbers[None, :, None])
    chosen_half = chosen.astype(jnp.bfloat16)
    piece = lax.all_gather(attended, "adapter", axis=0, tiled=True)
    product = lax.dot_general(
        piece, output_weight, (((1,), (1,)), ((), ())), preferred_element_type=jnp.float32
    )
    base_portion = product
    selected_rows = jnp.einsum(
        "ksn,nd->ksd", chosen_half, piece, preferred_element_type=jnp.float32
    ).astype(jnp.bfloat16)
    shrink_portion = jnp.einsum(
        "oij,omj->oim", selected_rows, adapter_down_weight, preferred_element_type=jnp.float32
    )
    base_portion, shrink_portion = (base_portion, shrink_portion)
    spread_rows = jnp.einsum(
        "ksn,ksr->nr", chosen.astype(jnp.float32), shrink_portion, precision=lax.Precision.HIGHEST
    )
    shrunk = lax.psum(spread_rows, ("adapter", "tensor")).astype(jnp.bfloat16)
    tensor_place = lax.axis_index("tensor")
    groups_number = adapter_up_weight.shape[1] // rank_width
    shifted = all_ids - tensor_place * groups_number
    block = min(batch_rows, 256)

    def expand(pair):
        ids_block, shrunk_block = pair
        hits = (ids_block[:, None] == jnp.arange(groups_number, dtype=jnp.int32)[None, :]).astype(
            jnp.bfloat16
        )
        expanded_update = (hits[:, :, None] * shrunk_block[:, None, :]).reshape(
            block, groups_number * rank_width
        )
        return lax.dot_general(
            expanded_update,
            adapter_up_weight,
            (((1,), (1,)), ((), ())),
            preferred_element_type=jnp.float32,
        )

    adapter_update = lax.map(
        expand,
        (
            shifted.reshape(batch_rows // block, block),
            shrunk.reshape(batch_rows // block, block, rank_width),
        ),
    )
    running_partial = base_portion + adapter_scale * adapter_update.reshape(
        batch_rows, column_width
    )
    blocks = lax.all_to_all(running_partial, "adapter", split_axis=0, concat_axis=1, tiled=True)
    total = lax.psum_scatter(blocks, "tensor", scatter_dimension=1, tiled=True)
    return total.astype(jnp.bfloat16)


def solution(mesh):
    sizes = mesh.shape
    direct = sizes["adapter"] <= 16 and sizes["tensor"] == 2
    in_specs = (
        P(("groups", "adapter"), "tensor"),
        P(("groups", "adapter"), None),
        P("adapter", "tensor"),
        P("adapter", None, "tensor"),
        P("adapter", "tensor"),
    )
    out_specs = P(("groups", "adapter"), "tensor")
    body = shards if direct else wide_shards
    return jax.shard_map(body, mesh=mesh, in_specs=in_specs, out_specs=out_specs, check_vma=False)
```

```python
import functools

import jax
import jax.numpy as jnp
from jax import lax
from jax.experimental import pallas as pl
from jax.experimental.pallas import tpu as pltpu
from jax.sharding import PartitionSpec as P

MOST = 8
LANES = 128
ID_BASE = 256
AHEAD = 40_000_000_000

adapter_scale = 2.0

f32, bf16, i32 = jnp.float32, jnp.bfloat16, jnp.int32
NT = (((1,), (1,)), ((), ()))
MIB = 1 << 20


def call(body, outs, args, vmem=4 * MIB, scratch=(), in_vmem=(), in_hbm=(), flops=0):
    args = [
        pltpu.with_memory_space_constraint(
            a, pltpu.VMEM if i in in_vmem else pltpu.HBM if i in in_hbm else pl.ANY
        )
        for i, a in enumerate(args)
    ]
    return pl.pallas_call(
        body,
        out_shape=outs,
        in_specs=[
            pl.BlockSpec(memory_space=pltpu.HBM if i in in_hbm else pltpu.VMEM)
            for i in range(len(args))
        ],
        out_specs=jax.tree.map(lambda _: pl.BlockSpec(memory_space=pltpu.VMEM), outs),
        scratch_shapes=list(scratch),
        compiler_params=pltpu.CompilerParams(vmem_limit_bytes=vmem),
        cost_estimate=pl.CostEstimate(flops=flops, bytes_accessed=flops // 100, transcendentals=0)
        if flops
        else None,
    )(*args)


def shape(*dims, dtype=f32):
    return jax.ShapeDtypeStruct(dims, dtype)


def iota(dims, axis):
    return lax.broadcasted_iota(i32, dims, axis)


def pack_kernel(att_hbm, ids_hbm, out_ref, att_ref, ids_ref, sems):
    copies = [
        pltpu.make_async_copy(att_hbm, att_ref, sems.at[0]),
        pltpu.make_async_copy(ids_hbm, ids_ref, sems.at[1]),
    ]
    for c in copies:
        c.start()
    for c in copies:
        c.wait()
    per_dev, width = att_ref.shape
    here = iota((per_dev, per_dev), 0) == iota((per_dev, per_dev), 1)
    ids = jnp.sum(jnp.where(here, ids_ref[...], 0), axis=1, keepdims=True)
    lane = iota((per_dev, LANES), 1)
    digits = jnp.where(lane == 0, ids >> 8, jnp.where(lane == 1, ids & (ID_BASE - 1), 0))
    out_ref[:, :width] = att_ref[...]
    out_ref[:, width:] = digits.astype(f32).astype(bf16)


def shrink_kernel(n, local, order, *refs):
    blocks = [refs[order.index(e)] for e in range(n)]
    down_ref, x_ref, meta_ref, slots_ref = refs[n + 1 :]
    per_dev = blocks[0].shape[0]
    width = x_ref.shape[1]
    rows = n * per_dev
    me = lax.axis_index("adapter")
    whole = jnp.concatenate([b[...].astype(f32) for b in blocks], axis=0)
    x_ref[...] = whole[:, :width].astype(bf16)
    product = lax.dot_general(x_ref[...], down_ref[...], NT, preferred_element_type=f32)
    digits = whole[:, width:]
    lane = iota((rows, LANES), 1)
    ids = jnp.sum(
        jnp.where(lane == 0, digits * ID_BASE, jnp.where(lane == 1, digits, 0.0)),
        axis=1,
        keepdims=True,
    ).astype(i32)
    square = (rows, rows)
    diagonal = iota(square, 0) == iota(square, 1)

    def home(which):
        return ((which // per_dev) ^ me) * per_dev + which % per_dev

    ids_across = jnp.sum(jnp.where(diagonal, ids, 0), axis=0, keepdims=True)
    same = ids == ids_across
    down_order, across_order = home(iota(square, 0)), home(iota(square, 1))
    rank = jnp.sum((same & (across_order < down_order)).astype(i32), axis=1, keepdims=True)
    rank_across = jnp.sum((same & (down_order < across_order)).astype(i32), axis=0, keepdims=True)
    meta_ref[...] = jnp.where(lane == 0, ids, rank)
    rank_width = down_ref.shape[0] // local
    slots = jnp.zeros((MOST, local * rank_width), f32)
    slot_lane = iota(slots.shape, 1)
    for k in range(local):
        picks = (rank_across == iota((MOST, rows), 0)) & (ids_across == me * local + k)
        found = jnp.dot(
            picks.astype(f32), product, precision=lax.Precision.HIGHEST, preferred_element_type=f32
        )
        slots = jnp.where(slot_lane // rank_width == k, found, slots)
    slots_ref[...] = slots


def base_kernel(place, x_ref, weight_ref, *refs):
    out_ref = refs[-1]
    width = out_ref.shape[1]
    out_ref[...] = lax.dot_general(
        x_ref[...],
        weight_ref[place * width : (place + 1) * width, :],
        NT,
        preferred_element_type=f32,
    )


def round_kernel(mine_ref, other_ref, across_ref, across_other_ref, *refs):
    out_ref = refs[-1]
    out_ref[0] = (mine_ref[...] + other_ref[...]).astype(bf16).astype(f32)
    out_ref[1] = (across_ref[...] + across_other_ref[...]).astype(bf16).astype(f32)


def near_place():
    part = lax.axis_size("adapter") // lax.axis_size("tensor")
    return lax.axis_index("tensor") == lax.axis_index("adapter") // part


def kept_rows(count, near):
    keep = jnp.where(near, 0, count)
    return pl.ds(pl.multiple_of(keep, count), count), pl.ds(
        pl.multiple_of(count - keep, count), count
    )


def split_kernel(*refs):
    parts, (keep_ref, give_ref) = refs[:-2], refs[-2:]
    keep, give = kept_rows(keep_ref.shape[0], near_place())
    at = 0
    for part in parts:
        columns = slice(at, at + part.shape[1])
        keep_ref[:, columns] = part[keep, :]
        give_ref[:, columns] = part[give, :]
        at += part.shape[1]


def update_kernel(part, local, rank_width, *refs):
    owners = refs[:part]
    meta_ref, up_ref, other_up_ref, out_ref, spread_ref = refs[part:]
    rows = out_ref.shape[0]
    me, core = lax.axis_index("adapter"), lax.axis_index("tensor")
    keep, _ = kept_rows(rows, near_place())
    meta = meta_ref[keep, :]
    ids, rank = meta[:, :1], meta[:, 1:2]
    picks = (rank == iota((rows, MOST), 1)).astype(f32).astype(bf16)
    wide = local * rank_width
    for e, slots_ref in enumerate(owners):
        for across in range(slots_ref.shape[0]):
            owner = me ^ (e + across * part)
            spread = jnp.dot(picks, slots_ref[across].astype(bf16), preferred_element_type=f32)
            wanted = iota(spread.shape, 1) // rank_width + owner * local
            at = pl.ds(pl.multiple_of(owner % part * wide, wide), wide)
            spread = jnp.where(ids == wanted, spread, 0.0).astype(bf16)
            spread_ref[owner // part, :, at] = spread
    update = lax.dot_general(spread_ref[core], up_ref[...], NT, preferred_element_type=f32)
    update += lax.dot_general(
        spread_ref[1 - core], other_up_ref[...], NT, preferred_element_type=f32
    )
    out_ref[...] = adapter_scale * update


def total_kernel(keep_ref, other_ref, update_ref, out_ref):
    per_dev = out_ref.shape[1]
    for e in range(out_ref.shape[0]):
        at = slice(e * per_dev, (e + 1) * per_dev)
        out_ref[e] = (keep_ref[at] + other_ref[at] + update_ref[at]).astype(bf16)


def unstack_kernel(mine_ref, across_ref, *out_refs):
    near = near_place()
    for m, out_ref in enumerate(out_refs):
        out_ref[...] = jnp.where(near, mine_ref[m].astype(f32), across_ref[m].astype(f32)).astype(
            bf16
        )


def join_kernel(*refs):
    (own_ref, *blocks), out_ref = refs[:-1], refs[-1]
    blocks = [own_ref, *reversed(blocks)]
    part, width = len(blocks), blocks[0].shape[1]
    low = lax.axis_index("adapter") % part
    for m, ref in enumerate(blocks):
        out_ref[:, pl.ds(pl.multiple_of((low ^ m) * width, width), width)] = ref[...]


def shards(attended, adapter_index_rows, output_weight, adapter_down_weight, adapter_up_weight):
    per_dev, half_width = attended.shape
    column_width = output_weight.shape[0]
    local, rank_width = adapter_down_weight.shape[:2]
    n = lax.axis_size("adapter")
    cores = lax.axis_size("tensor")
    part = n // cores
    rows = n * per_dev
    both = ("adapter", "tensor")

    def to(e, other):
        return [(i * cores + t, (i ^ e) * cores + (t ^ other)) for i in range(n) for t in range(cores)]

    other_up = lax.ppermute(adapter_up_weight, both, to(0, 1))
    payload = call(
        pack_kernel,
        shape(per_dev, half_width + LANES, dtype=bf16),
        [attended, adapter_index_rows.reshape(1, per_dev)],
        in_hbm=(0, 1),
        flops=AHEAD,
        scratch=[
            pltpu.VMEM((per_dev, half_width), bf16),
            pltpu.VMEM((1, per_dev), i32),
            pltpu.SemaphoreType.DMA((2,)),
        ],
    )
    blocks = [payload] * n
    for e in [*range(2, n, 2), *range(1, n, 2)]:
        if e % 2 == 0:
            blocks[e] = lax.ppermute(payload, "adapter", [(i, i ^ e) for i in range(n)])
        else:
            blocks[e] = lax.ppermute(blocks[e - 1], "adapter", [(i, i ^ 1) for i in range(n)])
    order = [0, 1, 4, 5, 2, 3, 6, 7] if n == 8 else list(range(n))
    down = adapter_down_weight.reshape(local * rank_width, half_width)
    piece, meta, slots = call(
        functools.partial(shrink_kernel, n, local, order),
        (
            shape(rows, half_width, dtype=bf16),
            shape(rows, LANES, dtype=i32),
            shape(MOST, local * rank_width),
        ),
        [blocks[e] for e in order] + [other_up, down],
        vmem=16 * MIB,
        in_vmem=(n,),
    )
    sections = 2

    def base_part(place, after=()):
        return call(
            functools.partial(base_kernel, place),
            shape(rows, column_width // sections),
            [piece, output_weight, *after],
            vmem=8 * MIB,
            in_vmem=(1,),
            flops=rows * column_width * half_width,
        )

    wide = local * rank_width
    sums = [
        lax.ppermute(slots, both, to(0, 1)),
        lax.ppermute(slots, both, to(part, 0)),
        lax.ppermute(slots, both, to(part, 1)),
    ]
    base = [base_part(0, sums[:1])]
    held = call(round_kernel, shape(cores, MOST, wide), [slots, *sums, *base])
    owners = [held] + [lax.ppermute(held, both, to(e, 0)) for e in range(1, part)]
    base += [base_part(place, owners[-1:]) for place in range(1, sections)]
    kept = shape(rows // cores, column_width)
    keep, give = call(split_kernel, (kept, kept), base)
    other = lax.ppermute(give, both, to(0, 1))
    update = call(
        functools.partial(update_kernel, part, local, rank_width),
        kept,
        [*owners, meta, adapter_up_weight, other_up],
        vmem=8 * MIB,
        in_vmem=(part + 1, part + 2),
        flops=4_000_000_000,
        scratch=[pltpu.VMEM((cores, rows // cores, part * wide), bf16)],
    )
    total = call(
        total_kernel, shape(part, per_dev, column_width, dtype=bf16), [keep, other, update]
    )
    across = lax.ppermute(total, both, to(part, 1))
    block = shape(per_dev, column_width, dtype=bf16)
    blocks = call(unstack_kernel, (block,) * part, [total, across])
    blocks = [v if m == 0 else lax.ppermute(v, both, to(m, 0)) for m, v in enumerate(blocks)]
    blocks[1:] = reversed(blocks[1:])
    return call(join_kernel, shape(per_dev, part * column_width, dtype=bf16), blocks)


def wide_shards(attended, adapter_index_rows, output_weight, adapter_down_weight, adapter_up_weight):
    per_dev = attended.shape[0]
    column_width = output_weight.shape[0]
    local_count = adapter_down_weight.shape[0]
    rank_width = adapter_down_weight.shape[1]
    owner = lax.axis_index("adapter")
    width_all = lax.axis_size("adapter")
    batch_rows = per_dev * width_all
    all_ids = lax.all_gather(adapter_index_rows, "adapter", axis=0, tiled=True)[:, 0]
    owned = owner * local_count + jnp.arange(local_count, dtype=jnp.int32)
    mine = (all_ids[None, :] == owned[:, None]).astype(jnp.int32)
    order_rank = jnp.cumsum(mine, axis=1) - 1
    slot_numbers = jnp.arange(MOST, dtype=jnp.int32)
    chosen = (mine[:, None, :] == 1) & (order_rank[:, None, :] == slot_numbers[None, :, None])
    chosen_half = chosen.astype(jnp.bfloat16)
    piece = lax.all_gather(attended, "adapter", axis=0, tiled=True)
    product = lax.dot_general(
        piece, output_weight, (((1,), (1,)), ((), ())), preferred_element_type=jnp.float32
    )
    base_portion = product
    selected_rows = jnp.einsum(
        "ksn,nd->ksd", chosen_half, piece, preferred_element_type=jnp.float32
    ).astype(jnp.bfloat16)
    shrink_portion = jnp.einsum(
        "oij,omj->oim", selected_rows, adapter_down_weight, preferred_element_type=jnp.float32
    )
    base_portion, shrink_portion = (base_portion, shrink_portion)
    spread_rows = jnp.einsum(
        "ksn,ksr->nr", chosen.astype(jnp.float32), shrink_portion, precision=lax.Precision.HIGHEST
    )
    shrunk = lax.psum(spread_rows, ("adapter", "tensor")).astype(jnp.bfloat16)
    tensor_place = lax.axis_index("tensor")
    groups_number = adapter_up_weight.shape[1] // rank_width
    shifted = all_ids - tensor_place * groups_number
    block = min(batch_rows, 256)

    def expand(pair):
        ids_block, shrunk_block = pair
        hits = (ids_block[:, None] == jnp.arange(groups_number, dtype=jnp.int32)[None, :]).astype(
            jnp.bfloat16
        )
        expanded_update = (hits[:, :, None] * shrunk_block[:, None, :]).reshape(
            block, groups_number * rank_width
        )
        return lax.dot_general(
            expanded_update,
            adapter_up_weight,
            (((1,), (1,)), ((), ())),
            preferred_element_type=jnp.float32,
        )

    adapter_update = lax.map(
        expand,
        (
            shifted.reshape(batch_rows // block, block),
            shrunk.reshape(batch_rows // block, block, rank_width),
        ),
    )
    running_partial = base_portion + adapter_scale * adapter_update.reshape(
        batch_rows, column_width
    )
    blocks = lax.all_to_all(running_partial, "adapter", split_axis=0, concat_axis=1, tiled=True)
    total = lax.psum_scatter(blocks, "tensor", scatter_dimension=1, tiled=True)
    return total.astype(jnp.bfloat16)


def solution(mesh):
    sizes = mesh.shape
    direct = sizes["adapter"] <= 16 and sizes["tensor"] == 2
    in_specs = (
        P(("groups", "adapter"), "tensor"),
        P(("groups", "adapter"), None),
        P("adapter", "tensor"),
        P("adapter", None, "tensor"),
        P("adapter", "tensor"),
    )
    out_specs = P(("groups", "adapter"), "tensor")
    body = shards if direct else wide_shards
    return jax.shard_map(body, mesh=mesh, in_specs=in_specs, out_specs=out_specs, check_vma=False)
```

```python
import functools

import jax
import jax.numpy as jnp
from jax import lax
from jax.experimental import pallas as pl
from jax.experimental.pallas import tpu as pltpu
from jax.sharding import PartitionSpec as P

MOST = 8
LANES = 128
ID_BASE = 256
AHEAD = 40_000_000_000

adapter_scale = 2.0

f32, bf16, i32 = jnp.float32, jnp.bfloat16, jnp.int32
NT = (((1,), (1,)), ((), ()))
MIB = 1 << 20


def call(body, outs, args, vmem=4 * MIB, scratch=(), in_vmem=(), in_hbm=(), flops=0):
    args = [
        pltpu.with_memory_space_constraint(
            a, pltpu.VMEM if i in in_vmem else pltpu.HBM if i in in_hbm else pl.ANY
        )
        for i, a in enumerate(args)
    ]
    return pl.pallas_call(
        body,
        out_shape=outs,
        in_specs=[
            pl.BlockSpec(memory_space=pltpu.HBM if i in in_hbm else pltpu.VMEM)
            for i in range(len(args))
        ],
        out_specs=jax.tree.map(lambda _: pl.BlockSpec(memory_space=pltpu.VMEM), outs),
        scratch_shapes=list(scratch),
        compiler_params=pltpu.CompilerParams(vmem_limit_bytes=vmem),
        cost_estimate=pl.CostEstimate(flops=flops, bytes_accessed=flops // 100, transcendentals=0)
        if flops
        else None,
    )(*args)


def shape(*dims, dtype=f32):
    return jax.ShapeDtypeStruct(dims, dtype)


def iota(dims, axis):
    return lax.broadcasted_iota(i32, dims, axis)


def pack_kernel(att_hbm, ids_hbm, out_ref, att_ref, ids_ref, sems):
    copies = [
        pltpu.make_async_copy(att_hbm, att_ref, sems.at[0]),
        pltpu.make_async_copy(ids_hbm, ids_ref, sems.at[1]),
    ]
    for c in copies:
        c.start()
    for c in copies:
        c.wait()
    per_dev, width = att_ref.shape
    here = iota((per_dev, per_dev), 0) == iota((per_dev, per_dev), 1)
    ids = jnp.sum(jnp.where(here, ids_ref[...], 0), axis=1, keepdims=True)
    lane = iota((per_dev, LANES), 1)
    digits = jnp.where(lane == 0, ids >> 8, jnp.where(lane == 1, ids & (ID_BASE - 1), 0))
    out_ref[:, :width] = att_ref[...]
    out_ref[:, width:] = digits.astype(f32).astype(bf16)


def shrink_kernel(n, local, order, *refs):
    blocks = [refs[order.index(e)] for e in range(n)]
    down_ref, x_ref, meta_ref, slots_ref = refs[n + 1 :]
    per_dev = blocks[0].shape[0]
    width = x_ref.shape[1]
    rows = n * per_dev
    me = lax.axis_index("adapter")
    whole = jnp.concatenate([b[...].astype(f32) for b in blocks], axis=0)
    x_ref[...] = whole[:, :width].astype(bf16)
    product = lax.dot_general(x_ref[...], down_ref[...], NT, preferred_element_type=f32)
    digits = whole[:, width:]
    lane = iota((rows, LANES), 1)
    ids = jnp.sum(
        jnp.where(lane == 0, digits * ID_BASE, jnp.where(lane == 1, digits, 0.0)),
        axis=1,
        keepdims=True,
    ).astype(i32)
    square = (rows, rows)
    diagonal = iota(square, 0) == iota(square, 1)

    def home(which):
        return ((which // per_dev) ^ me) * per_dev + which % per_dev

    ids_across = jnp.sum(jnp.where(diagonal, ids, 0), axis=0, keepdims=True)
    same = ids == ids_across
    down_order, across_order = home(iota(square, 0)), home(iota(square, 1))
    rank = jnp.sum((same & (across_order < down_order)).astype(i32), axis=1, keepdims=True)
    rank_across = jnp.sum((same & (down_order < across_order)).astype(i32), axis=0, keepdims=True)
    meta_ref[...] = jnp.where(lane == 0, ids, rank)
    rank_width = down_ref.shape[0] // local
    slots = jnp.zeros((MOST, local * rank_width), f32)
    slot_lane = iota(slots.shape, 1)
    for k in range(local):
        picks = (rank_across == iota((MOST, rows), 0)) & (ids_across == me * local + k)
        found = jnp.dot(
            picks.astype(f32), product, precision=lax.Precision.HIGHEST, preferred_element_type=f32
        )
        slots = jnp.where(slot_lane // rank_width == k, found, slots)
    slots_ref[...] = slots


def base_kernel(place, x_ref, weight_ref, *refs):
    out_ref = refs[-1]
    width = out_ref.shape[1]
    out_ref[...] = lax.dot_general(
        x_ref[...],
        weight_ref[place * width : (place + 1) * width, :],
        NT,
        preferred_element_type=f32,
    )


def round_kernel(mine_ref, other_ref, *refs):
    refs[-1][...] = (mine_ref[...] + other_ref[...]).astype(bf16).astype(f32)


def stack_kernel(mine_ref, across_ref, *refs):
    refs[-1][0] = mine_ref[...]
    refs[-1][1] = across_ref[...]


def near_place():
    part = lax.axis_size("adapter") // lax.axis_size("tensor")
    return lax.axis_index("tensor") == lax.axis_index("adapter") // part


def kept_rows(count, near):
    keep = jnp.where(near, 0, count)
    return pl.ds(pl.multiple_of(keep, count), count), pl.ds(
        pl.multiple_of(count - keep, count), count
    )


def split_kernel(*refs):
    parts, (keep_ref, give_ref) = refs[:-2], refs[-2:]
    keep, give = kept_rows(keep_ref.shape[0], near_place())
    at = 0
    for part in parts:
        columns = slice(at, at + part.shape[1])
        keep_ref[:, columns] = part[keep, :]
        give_ref[:, columns] = part[give, :]
        at += part.shape[1]


def update_kernel(part, local, rank_width, *refs):
    owners = refs[:part]
    meta_ref, up_ref, other_up_ref, out_ref, spread_ref = refs[part:]
    rows = out_ref.shape[0]
    me, core = lax.axis_index("adapter"), lax.axis_index("tensor")
    keep, _ = kept_rows(rows, near_place())
    meta = meta_ref[keep, :]
    ids, rank = meta[:, :1], meta[:, 1:2]
    picks = (rank == iota((rows, MOST), 1)).astype(f32).astype(bf16)
    wide = local * rank_width
    for e, slots_ref in enumerate(owners):
        for across in range(slots_ref.shape[0]):
            owner = me ^ (e + across * part)
            spread = jnp.dot(picks, slots_ref[across].astype(bf16), preferred_element_type=f32)
            wanted = iota(spread.shape, 1) // rank_width + owner * local
            at = pl.ds(pl.multiple_of(owner % part * wide, wide), wide)
            spread = jnp.where(ids == wanted, spread, 0.0).astype(bf16)
            spread_ref[owner // part, :, at] = spread
    update = lax.dot_general(spread_ref[core], up_ref[...], NT, preferred_element_type=f32)
    update += lax.dot_general(
        spread_ref[1 - core], other_up_ref[...], NT, preferred_element_type=f32
    )
    out_ref[...] = adapter_scale * update


def total_kernel(keep_ref, other_ref, update_ref, out_ref):
    per_dev = out_ref.shape[1]
    for e in range(out_ref.shape[0]):
        at = slice(e * per_dev, (e + 1) * per_dev)
        out_ref[e] = (keep_ref[at] + other_ref[at] + update_ref[at]).astype(bf16)


def unstack_kernel(stacked_ref, *out_refs):
    for m, out_ref in enumerate(out_refs):
        out_ref[...] = stacked_ref[m]


def join_kernel(*refs):
    (own_ref, *blocks), out_ref = refs[:-1], refs[-1]
    blocks = [own_ref, *reversed(blocks)]
    part, width = len(blocks), blocks[0].shape[1]
    low = lax.axis_index("adapter") % part
    for m, ref in enumerate(blocks):
        out_ref[:, pl.ds(pl.multiple_of((low ^ m) * width, width), width)] = ref[...]


def shards(attended, adapter_index_rows, output_weight, adapter_down_weight, adapter_up_weight):
    per_dev, half_width = attended.shape
    column_width = output_weight.shape[0]
    local, rank_width = adapter_down_weight.shape[:2]
    n = lax.axis_size("adapter")
    cores = lax.axis_size("tensor")
    part = n // cores
    rows = n * per_dev
    both = ("adapter", "tensor")

    def to(e, other):
        return [(i * cores + t, (i ^ e) * cores + (t ^ other)) for i in range(n) for t in range(cores)]

    other_up = lax.ppermute(adapter_up_weight, both, to(0, 1))
    payload = call(
        pack_kernel,
        shape(per_dev, half_width + LANES, dtype=bf16),
        [attended, adapter_index_rows.reshape(1, per_dev)],
        in_hbm=(0, 1),
        flops=AHEAD,
        scratch=[
            pltpu.VMEM((per_dev, half_width), bf16),
            pltpu.VMEM((1, per_dev), i32),
            pltpu.SemaphoreType.DMA((2,)),
        ],
    )
    blocks = [payload] * n
    for e in [*range(2, n, 2), *range(1, n, 2)]:
        if e % 2 == 0:
            blocks[e] = lax.ppermute(payload, "adapter", [(i, i ^ e) for i in range(n)])
        else:
            blocks[e] = lax.ppermute(blocks[e - 1], "adapter", [(i, i ^ 1) for i in range(n)])
    order = [0, 1, 4, 5, 2, 3, 6, 7] if n == 8 else list(range(n))
    down = adapter_down_weight.reshape(local * rank_width, half_width)
    piece, meta, slots = call(
        functools.partial(shrink_kernel, n, local, order),
        (
            shape(rows, half_width, dtype=bf16),
            shape(rows, LANES, dtype=i32),
            shape(MOST, local * rank_width),
        ),
        [blocks[e] for e in order] + [other_up, down],
        vmem=16 * MIB,
        in_vmem=(n,),
    )
    sections = 2

    def base_part(place, after=()):
        return call(
            functools.partial(base_kernel, place),
            shape(rows, column_width // sections),
            [piece, output_weight, *after],
            vmem=8 * MIB,
            in_vmem=(1,),
            flops=rows * column_width * half_width,
        )

    wide = local * rank_width
    other_slots = lax.ppermute(slots, both, to(0, 1))
    base_a = base_part(0)
    slots = call(round_kernel, shape(MOST, wide), [slots, other_slots, base_a])
    across_slots = lax.ppermute(slots, both, to(part, 0))
    base_b = base_part(1, [slots])
    held = call(stack_kernel, shape(cores, MOST, wide), [slots, across_slots, base_b])
    owners = [held] + [lax.ppermute(held, both, to(e, 0)) for e in range(1, part)]
    base = [base_a, base_b]
    kept = shape(rows // cores, column_width)
    keep, give = call(split_kernel, (kept, kept), base)
    other = lax.ppermute(give, both, to(0, 1))
    update = call(
        functools.partial(update_kernel, part, local, rank_width),
        kept,
        [*owners, meta, adapter_up_weight, other_up],
        vmem=8 * MIB,
        in_vmem=(part + 1, part + 2),
        flops=4_000_000_000,
        scratch=[pltpu.VMEM((cores, rows // cores, part * wide), bf16)],
    )
    total = call(
        total_kernel, shape(part, per_dev, column_width, dtype=bf16), [keep, other, update]
    )
    pairs = []
    for i in range(n):
        half = i // part
        pairs.append((i * cores + half, i * cores + half))
        pairs.append((i * cores + 1 - half, (i ^ part) * cores + half))
    total = lax.ppermute(total, both, pairs)
    block = shape(per_dev, column_width, dtype=bf16)
    blocks = call(unstack_kernel, (block,) * part, [total])
    blocks = [v if m == 0 else lax.ppermute(v, both, to(m, 0)) for m, v in enumerate(blocks)]
    blocks[1:] = reversed(blocks[1:])
    return call(join_kernel, shape(per_dev, part * column_width, dtype=bf16), blocks)


def wide_shards(attended, adapter_index_rows, output_weight, adapter_down_weight, adapter_up_weight):
    per_dev = attended.shape[0]
    column_width = output_weight.shape[0]
    local_count = adapter_down_weight.shape[0]
    rank_width = adapter_down_weight.shape[1]
    owner = lax.axis_index("adapter")
    width_all = lax.axis_size("adapter")
    batch_rows = per_dev * width_all
    all_ids = lax.all_gather(adapter_index_rows, "adapter", axis=0, tiled=True)[:, 0]
    owned = owner * local_count + jnp.arange(local_count, dtype=jnp.int32)
    mine = (all_ids[None, :] == owned[:, None]).astype(jnp.int32)
    order_rank = jnp.cumsum(mine, axis=1) - 1
    slot_numbers = jnp.arange(MOST, dtype=jnp.int32)
    chosen = (mine[:, None, :] == 1) & (order_rank[:, None, :] == slot_numbers[None, :, None])
    chosen_half = chosen.astype(jnp.bfloat16)
    piece = lax.all_gather(attended, "adapter", axis=0, tiled=True)
    product = lax.dot_general(
        piece, output_weight, (((1,), (1,)), ((), ())), preferred_element_type=jnp.float32
    )
    base_portion = product
    selected_rows = jnp.einsum(
        "ksn,nd->ksd", chosen_half, piece, preferred_element_type=jnp.float32
    ).astype(jnp.bfloat16)
    shrink_portion = jnp.einsum(
        "oij,omj->oim", selected_rows, adapter_down_weight, preferred_element_type=jnp.float32
    )
    base_portion, shrink_portion = (base_portion, shrink_portion)
    spread_rows = jnp.einsum(
        "ksn,ksr->nr", chosen.astype(jnp.float32), shrink_portion, precision=lax.Precision.HIGHEST
    )
    shrunk = lax.psum(spread_rows, ("adapter", "tensor")).astype(jnp.bfloat16)
    tensor_place = lax.axis_index("tensor")
    groups_number = adapter_up_weight.shape[1] // rank_width
    shifted = all_ids - tensor_place * groups_number
    block = min(batch_rows, 256)

    def expand(pair):
        ids_block, shrunk_block = pair
        hits = (ids_block[:, None] == jnp.arange(groups_number, dtype=jnp.int32)[None, :]).astype(
            jnp.bfloat16
        )
        expanded_update = (hits[:, :, None] * shrunk_block[:, None, :]).reshape(
            block, groups_number * rank_width
        )
        return lax.dot_general(
            expanded_update,
            adapter_up_weight,
            (((1,), (1,)), ((), ())),
            preferred_element_type=jnp.float32,
        )

    adapter_update = lax.map(
        expand,
        (
            shifted.reshape(batch_rows // block, block),
            shrunk.reshape(batch_rows // block, block, rank_width),
        ),
    )
    running_partial = base_portion + adapter_scale * adapter_update.reshape(
        batch_rows, column_width
    )
    blocks = lax.all_to_all(running_partial, "adapter", split_axis=0, concat_axis=1, tiled=True)
    total = lax.psum_scatter(blocks, "tensor", scatter_dimension=1, tiled=True)
    return total.astype(jnp.bfloat16)


def solution(mesh):
    sizes = mesh.shape
    direct = sizes["adapter"] <= 16 and sizes["tensor"] == 2
    in_specs = (
        P(("groups", "adapter"), "tensor"),
        P(("groups", "adapter"), None),
        P("adapter", "tensor"),
        P("adapter", None, "tensor"),
        P("adapter", "tensor"),
    )
    out_specs = P(("groups", "adapter"), "tensor")
    body = shards if direct else wide_shards
    return jax.shard_map(body, mesh=mesh, in_specs=in_specs, out_specs=out_specs, check_vma=False)
```

```python
import functools

import jax
import jax.numpy as jnp
from jax import lax
from jax.experimental import pallas as pl
from jax.experimental.pallas import tpu as pltpu
from jax.sharding import PartitionSpec as P

MOST = 8
LANES = 128
ID_BASE = 256
AHEAD = 40_000_000_000

adapter_scale = 2.0

f32, bf16, i32 = jnp.float32, jnp.bfloat16, jnp.int32
NT = (((1,), (1,)), ((), ()))
MIB = 1 << 20


def call(body, outs, args, vmem=4 * MIB, scratch=(), in_vmem=(), in_hbm=(), flops=0):
    args = [
        pltpu.with_memory_space_constraint(
            a, pltpu.VMEM if i in in_vmem else pltpu.HBM if i in in_hbm else pl.ANY
        )
        for i, a in enumerate(args)
    ]
    return pl.pallas_call(
        body,
        out_shape=outs,
        in_specs=[
            pl.BlockSpec(memory_space=pltpu.HBM if i in in_hbm else pltpu.VMEM)
            for i in range(len(args))
        ],
        out_specs=jax.tree.map(lambda _: pl.BlockSpec(memory_space=pltpu.VMEM), outs),
        scratch_shapes=list(scratch),
        compiler_params=pltpu.CompilerParams(vmem_limit_bytes=vmem),
        cost_estimate=pl.CostEstimate(flops=flops, bytes_accessed=flops // 100, transcendentals=0)
        if flops
        else None,
    )(*args)


def shape(*dims, dtype=f32):
    return jax.ShapeDtypeStruct(dims, dtype)


def iota(dims, axis):
    return lax.broadcasted_iota(i32, dims, axis)


def pack_kernel(att_hbm, ids_hbm, out_ref, att_ref, ids_ref, sems):
    copies = [
        pltpu.make_async_copy(att_hbm, att_ref, sems.at[0]),
        pltpu.make_async_copy(ids_hbm, ids_ref, sems.at[1]),
    ]
    for c in copies:
        c.start()
    for c in copies:
        c.wait()
    per_dev, width = att_ref.shape
    here = iota((per_dev, per_dev), 0) == iota((per_dev, per_dev), 1)
    ids = jnp.sum(jnp.where(here, ids_ref[...], 0), axis=1, keepdims=True)
    lane = iota((per_dev, LANES), 1)
    digits = jnp.where(lane == 0, ids >> 8, jnp.where(lane == 1, ids & (ID_BASE - 1), 0))
    out_ref[:, :width] = att_ref[...]
    out_ref[:, width:] = digits.astype(f32).astype(bf16)


def shrink_kernel(n, local, order, *refs):
    blocks = [refs[order.index(e)] for e in range(n)]
    down_ref, x_ref, meta_ref, slots_ref = refs[n + 1 :]
    per_dev = blocks[0].shape[0]
    width = x_ref.shape[1]
    rows = n * per_dev
    me = lax.axis_index("adapter")
    whole = jnp.concatenate([b[...].astype(f32) for b in blocks], axis=0)
    x_ref[...] = whole[:, :width].astype(bf16)
    product = lax.dot_general(x_ref[...], down_ref[...], NT, preferred_element_type=f32)
    digits = whole[:, width:]
    lane = iota((rows, LANES), 1)
    ids = jnp.sum(
        jnp.where(lane == 0, digits * ID_BASE, jnp.where(lane == 1, digits, 0.0)),
        axis=1,
        keepdims=True,
    ).astype(i32)
    square = (rows, rows)
    diagonal = iota(square, 0) == iota(square, 1)

    def home(which):
        return ((which // per_dev) ^ me) * per_dev + which % per_dev

    ids_across = jnp.sum(jnp.where(diagonal, ids, 0), axis=0, keepdims=True)
    same = ids == ids_across
    down_order, across_order = home(iota(square, 0)), home(iota(square, 1))
    rank = jnp.sum((same & (across_order < down_order)).astype(i32), axis=1, keepdims=True)
    rank_across = jnp.sum((same & (down_order < across_order)).astype(i32), axis=0, keepdims=True)
    meta_ref[...] = jnp.where(lane == 0, ids, rank)
    rank_width = down_ref.shape[0] // local
    slots = jnp.zeros((MOST, local * rank_width), f32)
    slot_lane = iota(slots.shape, 1)
    for k in range(local):
        picks = (rank_across == iota((MOST, rows), 0)) & (ids_across == me * local + k)
        found = jnp.dot(
            picks.astype(f32), product, precision=lax.Precision.HIGHEST, preferred_element_type=f32
        )
        slots = jnp.where(slot_lane // rank_width == k, found, slots)
    slots_ref[...] = slots


def base_kernel(place, x_ref, weight_ref, *refs):
    out_ref = refs[-1]
    width = out_ref.shape[1]
    out_ref[...] = lax.dot_general(
        x_ref[...],
        weight_ref[place * width : (place + 1) * width, :],
        NT,
        preferred_element_type=f32,
    )


def round_kernel(mine_ref, other_ref, *refs):
    refs[-1][...] = (mine_ref[...] + other_ref[...]).astype(bf16).astype(f32)


def stack_kernel(mine_ref, across_ref, *refs):
    refs[-1][0] = mine_ref[...]
    refs[-1][1] = across_ref[...]


def near_place():
    part = lax.axis_size("adapter") // lax.axis_size("tensor")
    return lax.axis_index("tensor") == lax.axis_index("adapter") // part


def kept_rows(quarter, near):
    starts = jnp.where(near, 0, quarter), jnp.where(near, 3 * quarter, 2 * quarter)
    return [pl.ds(pl.multiple_of(start, quarter), quarter) for start in starts]


def split_kernel(*refs):
    parts, (keep_ref, give_ref) = refs[:-2], refs[-2:]
    near = near_place()
    quarter = keep_ref.shape[0] // 2
    for out_ref, rows in (
        (keep_ref, kept_rows(quarter, near)),
        (give_ref, kept_rows(quarter, jnp.logical_not(near))),
    ):
        at = 0
        for part in parts:
            columns = slice(at, at + part.shape[1])
            for i, some in enumerate(rows):
                out_ref[i * quarter : (i + 1) * quarter, columns] = part[some, :]
            at += part.shape[1]


def update_kernel(part, local, rank_width, *refs):
    owners = refs[:part]
    meta_ref, up_ref, other_up_ref, out_ref, spread_ref = refs[part:]
    rows = out_ref.shape[0]
    me, core = lax.axis_index("adapter"), lax.axis_index("tensor")
    kept = kept_rows(rows // 2, near_place())
    meta = jnp.concatenate([meta_ref[some, :] for some in kept], axis=0)
    ids, rank = meta[:, :1], meta[:, 1:2]
    picks = (rank == iota((rows, MOST), 1)).astype(f32).astype(bf16)
    wide = local * rank_width
    for e, slots_ref in enumerate(owners):
        for across in range(slots_ref.shape[0]):
            owner = me ^ (e + across * part)
            spread = jnp.dot(picks, slots_ref[across].astype(bf16), preferred_element_type=f32)
            wanted = iota(spread.shape, 1) // rank_width + owner * local
            at = pl.ds(pl.multiple_of(owner % part * wide, wide), wide)
            spread = jnp.where(ids == wanted, spread, 0.0).astype(bf16)
            spread_ref[owner // part, :, at] = spread
    update = lax.dot_general(spread_ref[core], up_ref[...], NT, preferred_element_type=f32)
    update += lax.dot_general(
        spread_ref[1 - core], other_up_ref[...], NT, preferred_element_type=f32
    )
    out_ref[...] = adapter_scale * update


def total_kernel(keep_ref, other_ref, update_ref, *out_refs):
    at = 0
    for out_ref in out_refs:
        count, per_dev, _ = out_ref.shape
        for e in range(count):
            rows = slice(at, at + per_dev)
            out_ref[e] = (keep_ref[rows] + other_ref[rows] + update_ref[rows]).astype(bf16)
            at += per_dev


def choose_kernel(own_ref, across_ref, *out_refs):
    near = near_place()

    def put(*order):
        for out_ref, (ref, m) in zip(out_refs, order):
            out_ref[...] = ref[m]

    @pl.when(near)
    def _():
        put((own_ref, 0), (own_ref, 1), (across_ref, 0), (across_ref, 1))

    @pl.when(jnp.logical_not(near))
    def _():
        put((across_ref, 0), (across_ref, 1), (own_ref, 0), (own_ref, 1))


def join_kernel(*refs):
    (own_ref, *blocks), out_ref = refs[:-1], refs[-1]
    blocks = [own_ref, *reversed(blocks)]
    part, width = len(blocks), blocks[0].shape[1]
    low = lax.axis_index("adapter") % part
    for m, ref in enumerate(blocks):
        out_ref[:, pl.ds(pl.multiple_of((low ^ m) * width, width), width)] = ref[...]


def shards(attended, adapter_index_rows, output_weight, adapter_down_weight, adapter_up_weight):
    per_dev, half_width = attended.shape
    column_width = output_weight.shape[0]
    local, rank_width = adapter_down_weight.shape[:2]
    n = lax.axis_size("adapter")
    cores = lax.axis_size("tensor")
    part = n // cores
    rows = n * per_dev
    both = ("adapter", "tensor")

    def to(e, other):
        return [(i * cores + t, (i ^ e) * cores + (t ^ other)) for i in range(n) for t in range(cores)]

    other_up = lax.ppermute(adapter_up_weight, both, to(0, 1))
    payload = call(
        pack_kernel,
        shape(per_dev, half_width + LANES, dtype=bf16),
        [attended, adapter_index_rows.reshape(1, per_dev)],
        in_hbm=(0, 1),
        flops=AHEAD,
        scratch=[
            pltpu.VMEM((per_dev, half_width), bf16),
            pltpu.VMEM((1, per_dev), i32),
            pltpu.SemaphoreType.DMA((2,)),
        ],
    )
    blocks = [payload] * n
    for e in [*range(2, n, 2), *range(1, n, 2)]:
        if e % 2 == 0:
            blocks[e] = lax.ppermute(payload, "adapter", [(i, i ^ e) for i in range(n)])
        else:
            blocks[e] = lax.ppermute(blocks[e - 1], "adapter", [(i, i ^ 1) for i in range(n)])
    order = [0, 1, 4, 5, 2, 3, 6, 7] if n == 8 else list(range(n))
    down = adapter_down_weight.reshape(local * rank_width, half_width)
    piece, meta, slots = call(
        functools.partial(shrink_kernel, n, local, order),
        (
            shape(rows, half_width, dtype=bf16),
            shape(rows, LANES, dtype=i32),
            shape(MOST, local * rank_width),
        ),
        [blocks[e] for e in order] + [other_up, down],
        vmem=16 * MIB,
        in_vmem=(n,),
    )
    sections = 2

    def base_part(place, after=()):
        return call(
            functools.partial(base_kernel, place),
            shape(rows, column_width // sections),
            [piece, output_weight, *after],
            vmem=8 * MIB,
            in_vmem=(1,),
            flops=rows * column_width * half_width,
        )

    wide = local * rank_width
    other_slots = lax.ppermute(slots, both, to(0, 1))
    base_a = base_part(0)
    slots = call(round_kernel, shape(MOST, wide), [slots, other_slots, base_a])
    across_slots = lax.ppermute(slots, both, to(part, 0))
    base_b = base_part(1, [slots])
    held = call(stack_kernel, shape(cores, MOST, wide), [slots, across_slots, base_b])
    owners = [held] + [lax.ppermute(held, both, to(e, 0)) for e in range(1, part)]
    base = [base_a, base_b]
    kept = shape(rows // cores, column_width)
    keep, give = call(split_kernel, (kept, kept), base)
    other = lax.ppermute(give, both, to(0, 1))
    update = call(
        functools.partial(update_kernel, part, local, rank_width),
        kept,
        [*owners, meta, adapter_up_weight, other_up],
        vmem=8 * MIB,
        in_vmem=(part + 1, part + 2),
        flops=4_000_000_000,
        scratch=[pltpu.VMEM((cores, rows // cores, part * wide), bf16)],
    )
    pair = shape(part // 2, per_dev, column_width, dtype=bf16)
    own, across = call(total_kernel, (pair, pair), [keep, other, update])
    across = lax.ppermute(across, both, to(part, 1))
    block = shape(per_dev, column_width, dtype=bf16)
    blocks = list(call(choose_kernel, (block,) * part, [own, across]))
    for m in range(1, part):
        blocks[m] = lax.ppermute(blocks[m], both, to(m, m // 2))
    blocks[1:] = reversed(blocks[1:])
    return call(join_kernel, shape(per_dev, part * column_width, dtype=bf16), blocks)


def wide_shards(attended, adapter_index_rows, output_weight, adapter_down_weight, adapter_up_weight):
    per_dev = attended.shape[0]
    column_width = output_weight.shape[0]
    local_count = adapter_down_weight.shape[0]
    rank_width = adapter_down_weight.shape[1]
    owner = lax.axis_index("adapter")
    width_all = lax.axis_size("adapter")
    batch_rows = per_dev * width_all
    all_ids = lax.all_gather(adapter_index_rows, "adapter", axis=0, tiled=True)[:, 0]
    owned = owner * local_count + jnp.arange(local_count, dtype=jnp.int32)
    mine = (all_ids[None, :] == owned[:, None]).astype(jnp.int32)
    order_rank = jnp.cumsum(mine, axis=1) - 1
    slot_numbers = jnp.arange(MOST, dtype=jnp.int32)
    chosen = (mine[:, None, :] == 1) & (order_rank[:, None, :] == slot_numbers[None, :, None])
    chosen_half = chosen.astype(jnp.bfloat16)
    piece = lax.all_gather(attended, "adapter", axis=0, tiled=True)
    product = lax.dot_general(
        piece, output_weight, (((1,), (1,)), ((), ())), preferred_element_type=jnp.float32
    )
    base_portion = product
    selected_rows = jnp.einsum(
        "ksn,nd->ksd", chosen_half, piece, preferred_element_type=jnp.float32
    ).astype(jnp.bfloat16)
    shrink_portion = jnp.einsum(
        "oij,omj->oim", selected_rows, adapter_down_weight, preferred_element_type=jnp.float32
    )
    base_portion, shrink_portion = (base_portion, shrink_portion)
    spread_rows = jnp.einsum(
        "ksn,ksr->nr", chosen.astype(jnp.float32), shrink_portion, precision=lax.Precision.HIGHEST
    )
    shrunk = lax.psum(spread_rows, ("adapter", "tensor")).astype(jnp.bfloat16)
    tensor_place = lax.axis_index("tensor")
    groups_number = adapter_up_weight.shape[1] // rank_width
    shifted = all_ids - tensor_place * groups_number
    block = min(batch_rows, 256)

    def expand(pair):
        ids_block, shrunk_block = pair
        hits = (ids_block[:, None] == jnp.arange(groups_number, dtype=jnp.int32)[None, :]).astype(
            jnp.bfloat16
        )
        expanded_update = (hits[:, :, None] * shrunk_block[:, None, :]).reshape(
            block, groups_number * rank_width
        )
        return lax.dot_general(
            expanded_update,
            adapter_up_weight,
            (((1,), (1,)), ((), ())),
            preferred_element_type=jnp.float32,
        )

    adapter_update = lax.map(
        expand,
        (
            shifted.reshape(batch_rows // block, block),
            shrunk.reshape(batch_rows // block, block, rank_width),
        ),
    )
    running_partial = base_portion + adapter_scale * adapter_update.reshape(
        batch_rows, column_width
    )
    blocks = lax.all_to_all(running_partial, "adapter", split_axis=0, concat_axis=1, tiled=True)
    total = lax.psum_scatter(blocks, "tensor", scatter_dimension=1, tiled=True)
    return total.astype(jnp.bfloat16)


def solution(mesh):
    sizes = mesh.shape
    direct = sizes["adapter"] == 8 and sizes["tensor"] == 2
    in_specs = (
        P(("groups", "adapter"), "tensor"),
        P(("groups", "adapter"), None),
        P("adapter", "tensor"),
        P("adapter", None, "tensor"),
        P("adapter", "tensor"),
    )
    out_specs = P(("groups", "adapter"), "tensor")
    body = shards if direct else wide_shards
    return jax.shard_map(body, mesh=mesh, in_specs=in_specs, out_specs=out_specs, check_vma=False)
```

```python
import functools

import jax
import jax.numpy as jnp
from jax import lax
from jax.experimental import pallas as pl
from jax.experimental.pallas import tpu as pltpu
from jax.sharding import PartitionSpec as P

MOST = 8
LANES = 128
ID_BASE = 256
AHEAD = 40_000_000_000

adapter_scale = 2.0

f32, bf16, i32 = jnp.float32, jnp.bfloat16, jnp.int32
NT = (((1,), (1,)), ((), ()))
MIB = 1 << 20


def call(body, outs, args, vmem=4 * MIB, scratch=(), in_vmem=(), in_hbm=(), flops=0):
    args = [
        pltpu.with_memory_space_constraint(
            a, pltpu.VMEM if i in in_vmem else pltpu.HBM if i in in_hbm else pl.ANY
        )
        for i, a in enumerate(args)
    ]
    return pl.pallas_call(
        body,
        out_shape=outs,
        in_specs=[
            pl.BlockSpec(memory_space=pltpu.HBM if i in in_hbm else pltpu.VMEM)
            for i in range(len(args))
        ],
        out_specs=jax.tree.map(lambda _: pl.BlockSpec(memory_space=pltpu.VMEM), outs),
        scratch_shapes=list(scratch),
        compiler_params=pltpu.CompilerParams(vmem_limit_bytes=vmem),
        cost_estimate=pl.CostEstimate(flops=flops, bytes_accessed=flops // 100, transcendentals=0)
        if flops
        else None,
    )(*args)


def shape(*dims, dtype=f32):
    return jax.ShapeDtypeStruct(dims, dtype)


def iota(dims, axis):
    return lax.broadcasted_iota(i32, dims, axis)


def pack_kernel(att_hbm, ids_hbm, out_ref, att_ref, ids_ref, sems):
    copies = [
        pltpu.make_async_copy(att_hbm, att_ref, sems.at[0]),
        pltpu.make_async_copy(ids_hbm, ids_ref, sems.at[1]),
    ]
    for c in copies:
        c.start()
    for c in copies:
        c.wait()
    per_dev, width = att_ref.shape
    here = iota((per_dev, per_dev), 0) == iota((per_dev, per_dev), 1)
    ids = jnp.sum(jnp.where(here, ids_ref[...], 0), axis=1, keepdims=True)
    lane = iota((per_dev, LANES), 1)
    digits = jnp.where(lane == 0, ids >> 8, jnp.where(lane == 1, ids & (ID_BASE - 1), 0))
    out_ref[:, :width] = att_ref[...]
    out_ref[:, width:] = digits.astype(f32).astype(bf16)


def shrink_kernel(n, local, order, *refs):
    blocks = [refs[order.index(e)] for e in range(n)]
    down_ref, x_ref, meta_ref, slots_ref = refs[n + 1 :]
    per_dev = blocks[0].shape[0]
    width = x_ref.shape[1]
    rows = n * per_dev
    me = lax.axis_index("adapter")
    whole = jnp.concatenate([b[...].astype(f32) for b in blocks], axis=0)
    x_ref[...] = whole[:, :width].astype(bf16)
    product = lax.dot_general(x_ref[...], down_ref[...], NT, preferred_element_type=f32)
    digits = whole[:, width:]
    lane = iota((rows, LANES), 1)
    ids = jnp.sum(
        jnp.where(lane == 0, digits * ID_BASE, jnp.where(lane == 1, digits, 0.0)),
        axis=1,
        keepdims=True,
    ).astype(i32)
    square = (rows, rows)
    diagonal = iota(square, 0) == iota(square, 1)

    def home(which):
        return ((which // per_dev) ^ me) * per_dev + which % per_dev

    ids_across = jnp.sum(jnp.where(diagonal, ids, 0), axis=0, keepdims=True)
    same = ids == ids_across
    down_order, across_order = home(iota(square, 0)), home(iota(square, 1))
    rank = jnp.sum((same & (across_order < down_order)).astype(i32), axis=1, keepdims=True)
    rank_across = jnp.sum((same & (down_order < across_order)).astype(i32), axis=0, keepdims=True)
    meta_ref[...] = jnp.where(lane == 0, ids, rank)
    rank_width = down_ref.shape[0] // local
    slots = jnp.zeros((MOST, local * rank_width), f32)
    slot_lane = iota(slots.shape, 1)
    for k in range(local):
        picks = (rank_across == iota((MOST, rows), 0)) & (ids_across == me * local + k)
        found = jnp.dot(
            picks.astype(f32), product, precision=lax.Precision.HIGHEST, preferred_element_type=f32
        )
        slots = jnp.where(slot_lane // rank_width == k, found, slots)
    slots_ref[...] = slots


def base_kernel(place, x_ref, weight_ref, *refs):
    out_ref = refs[-1]
    width = out_ref.shape[1]
    out_ref[...] = lax.dot_general(
        x_ref[...],
        weight_ref[place * width : (place + 1) * width, :],
        NT,
        preferred_element_type=f32,
    )


def round_kernel(mine_ref, other_ref, *refs):
    refs[-1][...] = (mine_ref[...] + other_ref[...]).astype(bf16).astype(f32)


def stack_kernel(mine_ref, across_ref, *refs):
    refs[-1][0] = mine_ref[...]
    refs[-1][1] = across_ref[...]


def near_place():
    part = lax.axis_size("adapter") // lax.axis_size("tensor")
    return lax.axis_index("tensor") == lax.axis_index("adapter") // part


def kept_rows(quarter, near):
    starts = jnp.where(near, 0, quarter), jnp.where(near, 3 * quarter, 2 * quarter)
    return [pl.ds(pl.multiple_of(start, quarter), quarter) for start in starts]


def split_kernel(*refs):
    parts, (keep_ref, give_ref) = refs[:-2], refs[-2:]
    near = near_place()
    quarter = keep_ref.shape[0] // 2
    for out_ref, rows in (
        (keep_ref, kept_rows(quarter, near)),
        (give_ref, kept_rows(quarter, jnp.logical_not(near))),
    ):
        at = 0
        for part in parts:
            columns = slice(at, at + part.shape[1])
            for i, some in enumerate(rows):
                out_ref[i * quarter : (i + 1) * quarter, columns] = part[some, :]
            at += part.shape[1]


def update_kernel(part, local, rank_width, *refs):
    owners = refs[:part]
    meta_ref, up_ref, other_up_ref, out_ref, spread_ref = refs[part:]
    rows = out_ref.shape[0]
    me, core = lax.axis_index("adapter"), lax.axis_index("tensor")
    kept = kept_rows(rows // 2, near_place())
    meta = jnp.concatenate([meta_ref[some, :] for some in kept], axis=0)
    ids, rank = meta[:, :1], meta[:, 1:2]
    picks = (rank == iota((rows, MOST), 1)).astype(f32).astype(bf16)
    wide = local * rank_width
    for e, slots_ref in enumerate(owners):
        for across in range(slots_ref.shape[0]):
            owner = me ^ (e + across * part)
            spread = jnp.dot(picks, slots_ref[across].astype(bf16), preferred_element_type=f32)
            wanted = iota(spread.shape, 1) // rank_width + owner * local
            at = pl.ds(pl.multiple_of(owner % part * wide, wide), wide)
            spread = jnp.where(ids == wanted, spread, 0.0).astype(bf16)
            spread_ref[owner // part, :, at] = spread
    update = lax.dot_general(spread_ref[core], up_ref[...], NT, preferred_element_type=f32)
    update += lax.dot_general(
        spread_ref[1 - core], other_up_ref[...], NT, preferred_element_type=f32
    )
    out_ref[...] = adapter_scale * update


def total_kernel(keep_ref, other_ref, update_ref, *out_refs):
    at = 0
    for out_ref in out_refs:
        count, per_dev, _ = out_ref.shape
        for e in range(count):
            rows = slice(at, at + per_dev)
            out_ref[e] = (keep_ref[rows] + other_ref[rows] + update_ref[rows]).astype(bf16)
            at += per_dev


def choose_kernel(own_ref, across_ref, *out_refs):
    near = near_place()

    def put(*order):
        for out_ref, (ref, m) in zip(out_refs, order):
            out_ref[...] = ref[m]

    @pl.when(near)
    def _():
        put((own_ref, 0), (own_ref, 1), (across_ref, 0), (across_ref, 1))

    @pl.when(jnp.logical_not(near))
    def _():
        put((across_ref, 0), (across_ref, 1), (own_ref, 0), (own_ref, 1))


def join_kernel(*refs):
    (own_ref, *blocks), out_ref = refs[:-1], refs[-1]
    blocks = [own_ref, *reversed(blocks)]
    part, width = len(blocks), blocks[0].shape[1]
    low = lax.axis_index("adapter") % part
    for m, ref in enumerate(blocks):
        out_ref[:, pl.ds(pl.multiple_of((low ^ m) * width, width), width)] = ref[...]


def shards(attended, adapter_index_rows, output_weight, adapter_down_weight, adapter_up_weight):
    per_dev, half_width = attended.shape
    column_width = output_weight.shape[0]
    local, rank_width = adapter_down_weight.shape[:2]
    n = lax.axis_size("adapter")
    cores = lax.axis_size("tensor")
    part = n // cores
    rows = n * per_dev
    both = ("adapter", "tensor")

    def to(e, other):
        return [(i * cores + t, (i ^ e) * cores + (t ^ other)) for i in range(n) for t in range(cores)]

    other_up = lax.ppermute(adapter_up_weight, both, to(0, 1))
    payload = call(
        pack_kernel,
        shape(per_dev, half_width + LANES, dtype=bf16),
        [attended, adapter_index_rows.reshape(1, per_dev)],
        in_hbm=(0, 1),
        flops=AHEAD,
        scratch=[
            pltpu.VMEM((per_dev, half_width), bf16),
            pltpu.VMEM((1, per_dev), i32),
            pltpu.SemaphoreType.DMA((2,)),
        ],
    )
    blocks = [payload] * n
    for e in [*range(2, n, 2), *range(1, n, 2)]:
        if e % 2 == 0:
            blocks[e] = lax.ppermute(payload, "adapter", [(i, i ^ e) for i in range(n)])
        else:
            blocks[e] = lax.ppermute(blocks[e - 1], "adapter", [(i, i ^ 1) for i in range(n)])
    order = [0, 1, 4, 5, 2, 3, 6, 7] if n == 8 else list(range(n))
    down = adapter_down_weight.reshape(local * rank_width, half_width)
    piece, meta, slots = call(
        functools.partial(shrink_kernel, n, local, order),
        (
            shape(rows, half_width, dtype=bf16),
            shape(rows, LANES, dtype=i32),
            shape(MOST, local * rank_width),
        ),
        [blocks[e] for e in order] + [other_up, down],
        vmem=16 * MIB,
        in_vmem=(n,),
    )
    sections = 1

    def base_part(place, after=()):
        return call(
            functools.partial(base_kernel, place),
            shape(rows, column_width // sections),
            [piece, output_weight, *after],
            vmem=8 * MIB,
            in_vmem=(1,),
            flops=rows * column_width * half_width,
        )

    wide = local * rank_width
    other_slots = lax.ppermute(slots, both, to(0, 1))
    slots = call(round_kernel, shape(MOST, wide), [slots, other_slots])
    across_slots = lax.ppermute(slots, both, to(part, 0))
    base = [base_part(place, [slots]) for place in range(sections)]
    held = call(stack_kernel, shape(cores, MOST, wide), [slots, across_slots, *base])
    owners = [held] + [lax.ppermute(held, both, to(e, 0)) for e in range(1, part)]
    kept = shape(rows // cores, column_width)
    keep, give = call(split_kernel, (kept, kept), base)
    other = lax.ppermute(give, both, to(0, 1))
    update = call(
        functools.partial(update_kernel, part, local, rank_width),
        kept,
        [*owners, meta, adapter_up_weight, other_up],
        vmem=8 * MIB,
        in_vmem=(part + 1, part + 2),
        flops=4_000_000_000,
        scratch=[pltpu.VMEM((cores, rows // cores, part * wide), bf16)],
    )
    pair = shape(part // 2, per_dev, column_width, dtype=bf16)
    own, across = call(total_kernel, (pair, pair), [keep, other, update])
    across = lax.ppermute(across, both, to(part, 1))
    block = shape(per_dev, column_width, dtype=bf16)
    blocks = list(call(choose_kernel, (block,) * part, [own, across]))
    for m in range(1, part):
        blocks[m] = lax.ppermute(blocks[m], both, to(m, m // 2))
    blocks[1:] = reversed(blocks[1:])
    return call(join_kernel, shape(per_dev, part * column_width, dtype=bf16), blocks)


def wide_shards(attended, adapter_index_rows, output_weight, adapter_down_weight, adapter_up_weight):
    per_dev = attended.shape[0]
    column_width = output_weight.shape[0]
    local_count = adapter_down_weight.shape[0]
    rank_width = adapter_down_weight.shape[1]
    owner = lax.axis_index("adapter")
    width_all = lax.axis_size("adapter")
    batch_rows = per_dev * width_all
    all_ids = lax.all_gather(adapter_index_rows, "adapter", axis=0, tiled=True)[:, 0]
    owned = owner * local_count + jnp.arange(local_count, dtype=jnp.int32)
    mine = (all_ids[None, :] == owned[:, None]).astype(jnp.int32)
    order_rank = jnp.cumsum(mine, axis=1) - 1
    slot_numbers = jnp.arange(MOST, dtype=jnp.int32)
    chosen = (mine[:, None, :] == 1) & (order_rank[:, None, :] == slot_numbers[None, :, None])
    chosen_half = chosen.astype(jnp.bfloat16)
    piece = lax.all_gather(attended, "adapter", axis=0, tiled=True)
    product = lax.dot_general(
        piece, output_weight, (((1,), (1,)), ((), ())), preferred_element_type=jnp.float32
    )
    base_portion = product
    selected_rows = jnp.einsum(
        "ksn,nd->ksd", chosen_half, piece, preferred_element_type=jnp.float32
    ).astype(jnp.bfloat16)
    shrink_portion = jnp.einsum(
        "oij,omj->oim", selected_rows, adapter_down_weight, preferred_element_type=jnp.float32
    )
    base_portion, shrink_portion = (base_portion, shrink_portion)
    spread_rows = jnp.einsum(
        "ksn,ksr->nr", chosen.astype(jnp.float32), shrink_portion, precision=lax.Precision.HIGHEST
    )
    shrunk = lax.psum(spread_rows, ("adapter", "tensor")).astype(jnp.bfloat16)
    tensor_place = lax.axis_index("tensor")
    groups_number = adapter_up_weight.shape[1] // rank_width
    shifted = all_ids - tensor_place * groups_number
    block = min(batch_rows, 256)

    def expand(pair):
        ids_block, shrunk_block = pair
        hits = (ids_block[:, None] == jnp.arange(groups_number, dtype=jnp.int32)[None, :]).astype(
            jnp.bfloat16
        )
        expanded_update = (hits[:, :, None] * shrunk_block[:, None, :]).reshape(
            block, groups_number * rank_width
        )
        return lax.dot_general(
            expanded_update,
            adapter_up_weight,
            (((1,), (1,)), ((), ())),
            preferred_element_type=jnp.float32,
        )

    adapter_update = lax.map(
        expand,
        (
            shifted.reshape(batch_rows // block, block),
            shrunk.reshape(batch_rows // block, block, rank_width),
        ),
    )
    running_partial = base_portion + adapter_scale * adapter_update.reshape(
        batch_rows, column_width
    )
    blocks = lax.all_to_all(running_partial, "adapter", split_axis=0, concat_axis=1, tiled=True)
    total = lax.psum_scatter(blocks, "tensor", scatter_dimension=1, tiled=True)
    return total.astype(jnp.bfloat16)


def solution(mesh):
    sizes = mesh.shape
    direct = sizes["adapter"] == 8 and sizes["tensor"] == 2
    in_specs = (
        P(("groups", "adapter"), "tensor"),
        P(("groups", "adapter"), None),
        P("adapter", "tensor"),
        P("adapter", None, "tensor"),
        P("adapter", "tensor"),
    )
    out_specs = P(("groups", "adapter"), "tensor")
    body = shards if direct else wide_shards
    return jax.shard_map(body, mesh=mesh, in_specs=in_specs, out_specs=out_specs, check_vma=False)
```

```python
import functools

import jax
import jax.numpy as jnp
from jax import lax
from jax.experimental import pallas as pl
from jax.experimental.pallas import tpu as pltpu
from jax.sharding import PartitionSpec as P

MOST = 8
LANES = 128
ID_BASE = 256
AHEAD = 40_000_000_000

adapter_scale = 2.0

f32, bf16, i32 = jnp.float32, jnp.bfloat16, jnp.int32
NT = (((1,), (1,)), ((), ()))
MIB = 1 << 20


def call(body, outs, args, vmem=4 * MIB, scratch=(), in_vmem=(), in_hbm=(), flops=0):
    args = [
        pltpu.with_memory_space_constraint(
            a, pltpu.VMEM if i in in_vmem else pltpu.HBM if i in in_hbm else pl.ANY
        )
        for i, a in enumerate(args)
    ]
    return pl.pallas_call(
        body,
        out_shape=outs,
        in_specs=[
            pl.BlockSpec(memory_space=pltpu.HBM if i in in_hbm else pltpu.VMEM)
            for i in range(len(args))
        ],
        out_specs=jax.tree.map(lambda _: pl.BlockSpec(memory_space=pltpu.VMEM), outs),
        scratch_shapes=list(scratch),
        compiler_params=pltpu.CompilerParams(vmem_limit_bytes=vmem),
        cost_estimate=pl.CostEstimate(flops=flops, bytes_accessed=flops // 100, transcendentals=0)
        if flops
        else None,
    )(*args)


def shape(*dims, dtype=f32):
    return jax.ShapeDtypeStruct(dims, dtype)


def iota(dims, axis):
    return lax.broadcasted_iota(i32, dims, axis)


def pack_kernel(att_hbm, ids_hbm, out_ref, att_ref, ids_ref, sems):
    copies = [
        pltpu.make_async_copy(att_hbm, att_ref, sems.at[0]),
        pltpu.make_async_copy(ids_hbm, ids_ref, sems.at[1]),
    ]
    for c in copies:
        c.start()
    for c in copies:
        c.wait()
    per_dev, width = att_ref.shape
    here = iota((per_dev, per_dev), 0) == iota((per_dev, per_dev), 1)
    ids = jnp.sum(jnp.where(here, ids_ref[...], 0), axis=1, keepdims=True)
    lane = iota((per_dev, LANES), 1)
    digits = jnp.where(lane == 0, ids >> 8, jnp.where(lane == 1, ids & (ID_BASE - 1), 0))
    out_ref[:, :width] = att_ref[...]
    out_ref[:, width:] = digits.astype(f32).astype(bf16)


def shrink_kernel(n, local, order, *refs):
    blocks = [refs[order.index(e)] for e in range(n)]
    down_ref, x_ref, meta_ref, slots_ref = refs[n + 1 :]
    per_dev = blocks[0].shape[0]
    width = x_ref.shape[1]
    rows = n * per_dev
    me = lax.axis_index("adapter")
    whole = jnp.concatenate([b[...].astype(f32) for b in blocks], axis=0)
    x_ref[...] = whole[:, :width].astype(bf16)
    product = lax.dot_general(x_ref[...], down_ref[...], NT, preferred_element_type=f32)
    digits = whole[:, width:]
    lane = iota((rows, LANES), 1)
    ids = jnp.sum(
        jnp.where(lane == 0, digits * ID_BASE, jnp.where(lane == 1, digits, 0.0)),
        axis=1,
        keepdims=True,
    ).astype(i32)
    square = (rows, rows)
    diagonal = iota(square, 0) == iota(square, 1)

    def home(which):
        return ((which // per_dev) ^ me) * per_dev + which % per_dev

    ids_across = jnp.sum(jnp.where(diagonal, ids, 0), axis=0, keepdims=True)
    same = ids == ids_across
    down_order, across_order = home(iota(square, 0)), home(iota(square, 1))
    rank = jnp.sum((same & (across_order < down_order)).astype(i32), axis=1, keepdims=True)
    rank_across = jnp.sum((same & (down_order < across_order)).astype(i32), axis=0, keepdims=True)
    meta_ref[...] = jnp.where(lane == 0, ids, rank)
    rank_width = down_ref.shape[0] // local
    slots = jnp.zeros((MOST, local * rank_width), f32)
    slot_lane = iota(slots.shape, 1)
    for k in range(local):
        picks = (rank_across == iota((MOST, rows), 0)) & (ids_across == me * local + k)
        found = jnp.dot(
            picks.astype(f32), product, precision=lax.Precision.HIGHEST, preferred_element_type=f32
        )
        slots = jnp.where(slot_lane // rank_width == k, found, slots)
    slots_ref[...] = slots


def base_kernel(place, x_ref, weight_ref, *refs):
    out_ref = refs[-1]
    width = out_ref.shape[1]
    out_ref[...] = lax.dot_general(
        x_ref[...],
        weight_ref[place * width : (place + 1) * width, :],
        NT,
        preferred_element_type=f32,
    )


def round_kernel(mine_ref, other_ref, *refs):
    refs[-1][...] = (mine_ref[...] + other_ref[...]).astype(bf16).astype(f32)


def stack_kernel(mine_ref, across_ref, *refs):
    refs[-1][0] = mine_ref[...]
    refs[-1][1] = across_ref[...]


def near_place():
    part = lax.axis_size("adapter") // lax.axis_size("tensor")
    return lax.axis_index("tensor") == lax.axis_index("adapter") // part


def kept_rows(count, near):
    keep = jnp.where(near, 0, count)
    return pl.ds(pl.multiple_of(keep, count), count), pl.ds(
        pl.multiple_of(count - keep, count), count
    )


def split_kernel(*refs):
    parts, (keep_ref, give_ref) = refs[:-2], refs[-2:]
    keep, give = kept_rows(keep_ref.shape[0], near_place())
    at = 0
    for part in parts:
        columns = slice(at, at + part.shape[1])
        keep_ref[:, columns] = part[keep, :]
        give_ref[:, columns] = part[give, :]
        at += part.shape[1]


def update_kernel(part, local, rank_width, *refs):
    owners = refs[:part]
    meta_ref, up_ref, other_up_ref, out_ref, spread_ref = refs[part:]
    rows = out_ref.shape[0]
    me, core = lax.axis_index("adapter"), lax.axis_index("tensor")
    keep, _ = kept_rows(rows, near_place())
    meta = meta_ref[keep, :]
    ids, rank = meta[:, :1], meta[:, 1:2]
    picks = (rank == iota((rows, MOST), 1)).astype(f32).astype(bf16)
    wide = local * rank_width
    for e, slots_ref in enumerate(owners):
        for across in range(slots_ref.shape[0]):
            owner = me ^ (e + across * part)
            spread = jnp.dot(picks, slots_ref[across].astype(bf16), preferred_element_type=f32)
            wanted = iota(spread.shape, 1) // rank_width + owner * local
            at = pl.ds(pl.multiple_of(owner % part * wide, wide), wide)
            spread = jnp.where(ids == wanted, spread, 0.0).astype(bf16)
            spread_ref[owner // part, :, at] = spread
    update = lax.dot_general(spread_ref[core], up_ref[...], NT, preferred_element_type=f32)
    update += lax.dot_general(
        spread_ref[1 - core], other_up_ref[...], NT, preferred_element_type=f32
    )
    out_ref[...] = adapter_scale * update


def total_kernel(keep_ref, other_ref, update_ref, out_ref):
    per_dev = out_ref.shape[1]
    for e in range(out_ref.shape[0]):
        at = slice(e * per_dev, (e + 1) * per_dev)
        out_ref[e] = (keep_ref[at] + other_ref[at] + update_ref[at]).astype(bf16)


def unstack_kernel(stacked_ref, *out_refs):
    for m, out_ref in enumerate(out_refs):
        out_ref[...] = stacked_ref[m]


def join_kernel(*refs):
    (own_ref, *blocks), out_ref = refs[:-1], refs[-1]
    blocks = [own_ref, *reversed(blocks)]
    part, width = len(blocks), blocks[0].shape[1]
    low = lax.axis_index("adapter") % part
    for m, ref in enumerate(blocks):
        out_ref[:, pl.ds(pl.multiple_of((low ^ m) * width, width), width)] = ref[...]


def shards(attended, adapter_index_rows, output_weight, adapter_down_weight, adapter_up_weight):
    per_dev, half_width = attended.shape
    column_width = output_weight.shape[0]
    local, rank_width = adapter_down_weight.shape[:2]
    n = lax.axis_size("adapter")
    cores = lax.axis_size("tensor")
    part = n // cores
    rows = n * per_dev
    both = ("adapter", "tensor")

    def to(e, other):
        return [(i * cores + t, (i ^ e) * cores + (t ^ other)) for i in range(n) for t in range(cores)]

    other_up = lax.ppermute(adapter_up_weight, both, to(0, 1))
    payload = call(
        pack_kernel,
        shape(per_dev, half_width + LANES, dtype=bf16),
        [attended, adapter_index_rows.reshape(1, per_dev)],
        in_hbm=(0, 1),
        flops=AHEAD,
        scratch=[
            pltpu.VMEM((per_dev, half_width), bf16),
            pltpu.VMEM((1, per_dev), i32),
            pltpu.SemaphoreType.DMA((2,)),
        ],
    )
    blocks = [payload] * n
    for e in [*range(2, n, 2), *range(1, n, 2)]:
        if e % 2 == 0:
            blocks[e] = lax.ppermute(payload, "adapter", [(i, i ^ e) for i in range(n)])
        else:
            blocks[e] = lax.ppermute(blocks[e - 1], "adapter", [(i, i ^ 1) for i in range(n)])
    order = [0, 1, 4, 5, 2, 3, 6, 7] if n == 8 else list(range(n))
    down = adapter_down_weight.reshape(local * rank_width, half_width)
    piece, meta, slots = call(
        functools.partial(shrink_kernel, n, local, order),
        (
            shape(rows, half_width, dtype=bf16),
            shape(rows, LANES, dtype=i32),
            shape(MOST, local * rank_width),
        ),
        [blocks[e] for e in order] + [other_up, down],
        vmem=16 * MIB,
        in_vmem=(n,),
    )
    sections = 1

    def base_part(place, after=()):
        return call(
            functools.partial(base_kernel, place),
            shape(rows, column_width // sections),
            [piece, output_weight, *after],
            vmem=8 * MIB,
            in_vmem=(1,),
            flops=rows * column_width * half_width,
        )

    wide = local * rank_width
    other_slots = lax.ppermute(slots, both, to(0, 1))
    slots = call(round_kernel, shape(MOST, wide), [slots, other_slots])
    across_slots = lax.ppermute(slots, both, to(part, 0))
    base = [base_part(place, [slots]) for place in range(sections)]
    held = call(stack_kernel, shape(cores, MOST, wide), [slots, across_slots, *base])
    owners = [held] + [lax.ppermute(held, both, to(e, 0)) for e in range(1, part)]
    kept = shape(rows // cores, column_width)
    keep, give = call(split_kernel, (kept, kept), base)
    other = lax.ppermute(give, both, to(0, 1))
    update = call(
        functools.partial(update_kernel, part, local, rank_width),
        kept,
        [*owners, meta, adapter_up_weight, other_up],
        vmem=8 * MIB,
        in_vmem=(part + 1, part + 2),
        flops=4_000_000_000,
        scratch=[pltpu.VMEM((cores, rows // cores, part * wide), bf16)],
    )
    total = call(
        total_kernel, shape(part, per_dev, column_width, dtype=bf16), [keep, other, update]
    )
    pairs = []
    for i in range(n):
        half = i // part
        pairs.append((i * cores + half, i * cores + half))
        pairs.append((i * cores + 1 - half, (i ^ part) * cores + half))
    total = lax.ppermute(total, both, pairs)
    block = shape(per_dev, column_width, dtype=bf16)
    blocks = call(unstack_kernel, (block,) * part, [total])
    blocks = [v if m == 0 else lax.ppermute(v, both, to(m, 0)) for m, v in enumerate(blocks)]
    blocks[1:] = reversed(blocks[1:])
    return call(join_kernel, shape(per_dev, part * column_width, dtype=bf16), blocks)


def wide_shards(attended, adapter_index_rows, output_weight, adapter_down_weight, adapter_up_weight):
    per_dev = attended.shape[0]
    column_width = output_weight.shape[0]
    local_count = adapter_down_weight.shape[0]
    rank_width = adapter_down_weight.shape[1]
    owner = lax.axis_index("adapter")
    width_all = lax.axis_size("adapter")
    batch_rows = per_dev * width_all
    all_ids = lax.all_gather(adapter_index_rows, "adapter", axis=0, tiled=True)[:, 0]
    owned = owner * local_count + jnp.arange(local_count, dtype=jnp.int32)
    mine = (all_ids[None, :] == owned[:, None]).astype(jnp.int32)
    order_rank = jnp.cumsum(mine, axis=1) - 1
    slot_numbers = jnp.arange(MOST, dtype=jnp.int32)
    chosen = (mine[:, None, :] == 1) & (order_rank[:, None, :] == slot_numbers[None, :, None])
    chosen_half = chosen.astype(jnp.bfloat16)
    piece = lax.all_gather(attended, "adapter", axis=0, tiled=True)
    product = lax.dot_general(
        piece, output_weight, (((1,), (1,)), ((), ())), preferred_element_type=jnp.float32
    )
    base_portion = product
    selected_rows = jnp.einsum(
        "ksn,nd->ksd", chosen_half, piece, preferred_element_type=jnp.float32
    ).astype(jnp.bfloat16)
    shrink_portion = jnp.einsum(
        "oij,omj->oim", selected_rows, adapter_down_weight, preferred_element_type=jnp.float32
    )
    base_portion, shrink_portion = (base_portion, shrink_portion)
    spread_rows = jnp.einsum(
        "ksn,ksr->nr", chosen.astype(jnp.float32), shrink_portion, precision=lax.Precision.HIGHEST
    )
    shrunk = lax.psum(spread_rows, ("adapter", "tensor")).astype(jnp.bfloat16)
    tensor_place = lax.axis_index("tensor")
    groups_number = adapter_up_weight.shape[1] // rank_width
    shifted = all_ids - tensor_place * groups_number
    block = min(batch_rows, 256)

    def expand(pair):
        ids_block, shrunk_block = pair
        hits = (ids_block[:, None] == jnp.arange(groups_number, dtype=jnp.int32)[None, :]).astype(
            jnp.bfloat16
        )
        expanded_update = (hits[:, :, None] * shrunk_block[:, None, :]).reshape(
            block, groups_number * rank_width
        )
        return lax.dot_general(
            expanded_update,
            adapter_up_weight,
            (((1,), (1,)), ((), ())),
            preferred_element_type=jnp.float32,
        )

    adapter_update = lax.map(
        expand,
        (
            shifted.reshape(batch_rows // block, block),
            shrunk.reshape(batch_rows // block, block, rank_width),
        ),
    )
    running_partial = base_portion + adapter_scale * adapter_update.reshape(
        batch_rows, column_width
    )
    blocks = lax.all_to_all(running_partial, "adapter", split_axis=0, concat_axis=1, tiled=True)
    total = lax.psum_scatter(blocks, "tensor", scatter_dimension=1, tiled=True)
    return total.astype(jnp.bfloat16)


def solution(mesh):
    sizes = mesh.shape
    direct = sizes["adapter"] == 8 and sizes["tensor"] == 2
    in_specs = (
        P(("groups", "adapter"), "tensor"),
        P(("groups", "adapter"), None),
        P("adapter", "tensor"),
        P("adapter", None, "tensor"),
        P("adapter", "tensor"),
    )
    out_specs = P(("groups", "adapter"), "tensor")
    body = shards if direct else wide_shards
    return jax.shard_map(body, mesh=mesh, in_specs=in_specs, out_specs=out_specs, check_vma=False)
```
